128 devices in a mesh: row: 16 (over y_hi, x, core), col: 8 (over z, y_lo).
Axes of the slice: x: 4, y: 4 (y_hi: 2, y_lo: 2; y = y_hi * 2 + y_lo), z: 4, core: 2. Of those that a mesh axis runs over, the one named last changes fastest.
Arguments:
- cycle_inter: float32 [1536, 1536, 128], P(None, ('row', 'col')), may hold values from -6 to 6
- integrals: float32 [1536, 1536, 128], P(None, ('row', 'col')), may hold values from -0.005859375 to 0.005859375
Outputs:
- ladder: float32 [128, 128], P('row')
The draws below stay inside these ranges and needn't reach their ends.
All inputs are finite; a program needn't handle non-finite values.
Results may differ from the reference program's by a relative error of at most 0.0003.
Values sent between devices are 32-bit elements; how exact they have to be, the bound alone decides.
No kernel may reach another device: no remote copies, remote signals or barrier semaphores. Data moves between devices by JAX's collectives and lax.ppermute only.
A program may use at most 128 MiB of HBM per device.

```python
import jax
import jax.numpy as jnp
from jax import lax

NV = 1536
NOP = 128
AB = 128


def block_scale(stream_key, extent, cuts, smallest, high):
    loudness = 1.0
    for position, shards_of in cuts:
        heights = jax.random.uniform(jax.random.fold_in(jax.random.fold_in(stream_key, 6), position), (shards_of,), jnp.float32, smallest / len(cuts), high / len(cuts))
        loudness = loudness * jnp.repeat(jnp.exp(heights), extent[position] // shards_of).reshape((-1,) + (1,) * (len(extent) - 1 - position))
    return loudness


def bell_draw(stream_key, shape, spread, reach, shards=(), kind=jnp.bfloat16):
    loudness = block_scale(stream_key, shape, shards, -0.22, 0.18) if shards else 1.0
    drawn = jax.random.normal(stream_key, shape, jnp.float32) * spread * loudness
    return jnp.minimum(jnp.maximum(drawn, -reach), reach).astype(kind)


def setup_inputs(seed: int = 0) -> dict:
    seeds = jax.random.split(jax.random.key(seed), 3)
    return {
        "cycle_inter": bell_draw(seeds[0], (NV, NV, NOP), 1.0, 6.0, ((1, 128),), jnp.float32),
        "integrals": bell_draw(seeds[1], (NV, NV, AB), (NV * NV // 2) ** -0.5, 0.005859375, ((1, 128),), jnp.float32),
    }


def reference(cycle_inter, integrals):
    block_rows = 128
    block_count = NV // block_rows
    row_index = jnp.arange(NV, dtype=jnp.int32)

    def advance(summed, block_index):
        offset = (block_index * block_rows).astype(jnp.int32)
        direct = lax.dynamic_slice_in_dim(cycle_inter, offset, block_rows, 1)
        mirror = jnp.swapaxes(lax.dynamic_slice_in_dim(cycle_inter, offset, block_rows, 0), 0, 1)
        amplitudes = direct - mirror
        column_ids = offset + jnp.arange(block_rows, dtype=jnp.int32)
        upper_mask = (row_index[:, None] < column_ids[None, :]).astype(jnp.float32)
        amplitudes = amplitudes * upper_mask[:, :, None]
        integral_block = lax.dynamic_slice_in_dim(integrals, offset, block_rows, 1)
        summed = summed + jnp.einsum("cdi,cda->ia", amplitudes, integral_block, precision=lax.Precision.HIGHEST)
        return summed, None

    summed, _ = lax.scan(advance, jnp.zeros((NOP, AB), jnp.float32), jnp.arange(block_count, dtype=jnp.int32))
    return summed
```

```python
import functools

import jax
import jax.numpy as jnp
from jax import lax
from jax.experimental import pallas as pl
from jax.experimental.pallas import tpu as pltpu
from jax.sharding import PartitionSpec as P

AXES = ("row", "col")
DEVICES = 128
WIDTH = 12
HALF = WIDTH // 2
BLOCK = WIDTH * HALF
LANES = 128
PEERS = 16
GROUPS = DEVICES // PEERS
ROWS = PEERS * WIDTH
TERMS = PEERS * BLOCK
ROW_DEVICES = 16
COL_DEVICES = 8
OUT_ROWS = LANES // ROW_DEVICES
VMEM_LIMIT = 56 * 1024 * 1024


def split(value):
    high = value.astype(jnp.bfloat16)
    low = (value - high.astype(jnp.float32)).astype(jnp.bfloat16)
    return high, low


def dot(a, b):
    return lax.dot_general(a, b, (((1,), (0,)), ((), ())), preferred_element_type=jnp.float32)


def fold(acc):
    top = acc[:LANES, :LANES] + acc[:LANES, LANES:]
    return top + (acc[LANES:, :LANES] + acc[LANES:, LANES:])


def pack_kernel(rank_ref, x_ref, v_ref, out_ref):
    rank = rank_ref[0]
    group = pl.program_id(0)
    for i in range(PEERS):
        peer = group * PEERS + i

        @pl.when(peer > rank)
        def _():
            for c in range(HALF):
                out_ref[i, pl.ds(WIDTH * c, WIDTH), :] = x_ref[c, pl.ds(WIDTH * i, WIDTH), :]

        @pl.when(peer < rank)
        def _():
            for d in range(WIDTH):
                out_ref[i, pl.ds(HALF * d, HALF), :] = v_ref[d, pl.ds(WIDTH * i + HALF, HALF), :]

        @pl.when(peer == rank)
        def _():
            out_ref[i] = jnp.zeros((BLOCK, LANES), jnp.float32)


def pack(rank, x, v):
    return pl.pallas_call(
        pack_kernel,
        grid_spec=pltpu.PrefetchScalarGridSpec(
            num_scalar_prefetch=1,
            grid=(GROUPS,),
            in_specs=[
                pl.BlockSpec((HALF, ROWS, LANES), lambda g, r: (0, jnp.maximum(g, r[0] // PEERS), 0)),
                pl.BlockSpec((WIDTH, ROWS, LANES), lambda g, r: (0, jnp.minimum(g, r[0] // PEERS), 0)),
            ],
            out_specs=pl.BlockSpec((PEERS, BLOCK, LANES), lambda g, r: (g, 0, 0)),
        ),
        out_shape=jax.ShapeDtypeStruct((DEVICES, BLOCK, LANES), jnp.float32),
        compiler_params=pltpu.CompilerParams(vmem_limit_bytes=VMEM_LIMIT),
        cost_estimate=pl.CostEstimate(flops=0, bytes_accessed=12_000_000, transcendentals=0),
        name="pack",
    )(rank, x, v)


def local_kernel(rank_ref, x_ref, v_ref, left_ref, direct_ref, terms_ref, own_x_ref, own_v_ref, acc_ref):
    rank = rank_ref[0]
    group = pl.program_id(0)
    own_group = rank // PEERS

    @pl.when(group == 0)
    def _():
        acc_ref[...] = jnp.zeros_like(acc_ref)

    for i in range(PEERS):
        peer = group * PEERS + i

        @pl.when(peer > rank)
        def _():
            for c in range(HALF):
                terms_ref[pl.ds(BLOCK * i + c, WIDTH, stride=HALF), :] = x_ref[HALF + c, pl.ds(WIDTH * i, WIDTH), :]

        @pl.when(peer < rank)
        def _():
            for d in range(WIDTH):
                terms_ref[pl.ds(BLOCK * i + d, HALF, stride=WIDTH), :] = v_ref[d, pl.ds(WIDTH * i, HALF), :]

        @pl.when(peer == rank)
        def _():
            terms_ref[pl.ds(BLOCK * i, BLOCK), :] = jnp.zeros((BLOCK, LANES), jnp.float32)
            for c in range(WIDTH):
                own_x_ref[pl.ds(WIDTH * c, WIDTH), :] = x_ref[c, pl.ds(WIDTH * i, WIDTH), :]
                own_v_ref[pl.ds(c, WIDTH, stride=WIDTH), :] = v_ref[c, pl.ds(WIDTH * i, WIDTH), :]

    high, low = split(terms_ref[...].T)
    left_ref[0, :LANES, :] = high
    left_ref[0, LANES:, :] = low

    def add(x_rows, v_rows):
        left = jnp.concatenate(split(x_rows.T), axis=0)
        right = jnp.concatenate(split(v_rows), axis=1)
        acc_ref[...] += dot(left, right)

    @pl.when(group < own_group)
    def _():
        for d in range(WIDTH):
            add(x_ref[d], v_ref[d])

    @pl.when(group == own_group)
    def _():
        ids = group * ROWS + lax.broadcasted_iota(jnp.int32, (ROWS, LANES), 0)
        for d in range(WIDTH):
            add(x_ref[d], jnp.where(ids < rank * WIDTH + d, v_ref[d], 0.0))
        pair = lax.broadcasted_iota(jnp.int32, (WIDTH * WIDTH, LANES), 0)
        upper = pair % WIDTH > pair // WIDTH
        add(own_x_ref[...], jnp.where(upper, -own_v_ref[...], 0.0))

    @pl.when(group == GROUPS - 1)
    def _():
        direct_ref[...] = fold(acc_ref[...])


def local(rank, x, v):
    return pl.pallas_call(
        local_kernel,
        grid_spec=pltpu.PrefetchScalarGridSpec(
            num_scalar_prefetch=1,
            grid=(GROUPS,),
            in_specs=[
                pl.BlockSpec((WIDTH, ROWS, LANES), lambda g, r: (0, g, 0)),
                pl.BlockSpec((WIDTH, ROWS, LANES), lambda g, r: (0, jnp.minimum(g, r[0] // PEERS), 0)),
            ],
            out_specs=[
                pl.BlockSpec((1, 2 * LANES, TERMS), lambda g, r: (g, 0, 0)),
                pl.BlockSpec((LANES, LANES), lambda g, r: (0, 0)),
            ],
            scratch_shapes=[
                pltpu.VMEM((TERMS, LANES), jnp.float32),
                pltpu.VMEM((WIDTH * WIDTH, LANES), jnp.float32),
                pltpu.VMEM((WIDTH * WIDTH, LANES), jnp.float32),
                pltpu.VMEM((2 * LANES, 2 * LANES), jnp.float32),
            ],
        ),
        out_shape=[
            jax.ShapeDtypeStruct((GROUPS, 2 * LANES, TERMS), jnp.bfloat16),
            jax.ShapeDtypeStruct((LANES, LANES), jnp.float32),
        ],
        compiler_params=pltpu.CompilerParams(vmem_limit_bytes=VMEM_LIMIT),
        cost_estimate=pl.CostEstimate(flops=20_000_000_000, bytes_accessed=30_000_000, transcendentals=0),
        name="local",
    )(rank, x, v)


def mirror_kernel(rank_ref, left_ref, received_ref, direct_ref, out_ref, below_ref, above_ref):
    rank = rank_ref[0]
    group = pl.program_id(0)
    own_group = rank // PEERS

    @pl.when(group == 0)
    def _():
        below_ref[...] = jnp.zeros_like(below_ref)
        above_ref[...] = jnp.zeros_like(above_ref)

    def product(received):
        right = jnp.concatenate(split(received), axis=1)
        return dot(left_ref[0], right)

    received = received_ref[...].reshape(TERMS, LANES)

    @pl.when(group < own_group)
    def _():
        below_ref[...] += product(received)

    @pl.when(group > own_group)
    def _():
        above_ref[...] += product(received)

    @pl.when(group == own_group)
    def _():
        term = lax.broadcasted_iota(jnp.int32, (TERMS, LANES), 0)
        first = (rank - group * PEERS) * BLOCK
        below_ref[...] += product(jnp.where(term < first, received, 0.0))
        above_ref[...] += product(jnp.where(term >= first + BLOCK, received, 0.0))

    @pl.when(group == GROUPS - 1)
    def _():
        total = direct_ref[...] - (fold(above_ref[...]) + fold(below_ref[...]).T)
        for row in range(ROW_DEVICES):
            rows = total[OUT_ROWS * row : OUT_ROWS * (row + 1), :]
            for col in range(COL_DEVICES):
                out_ref[COL_DEVICES * row + col] = rows


def mirror(rank, left, received, direct):
    return pl.pallas_call(
        mirror_kernel,
        grid_spec=pltpu.PrefetchScalarGridSpec(
            num_scalar_prefetch=1,
            grid=(GROUPS,),
            in_specs=[
                pl.BlockSpec((1, 2 * LANES, TERMS), lambda g, r: (g, 0, 0)),
                pl.BlockSpec((PEERS, BLOCK, LANES), lambda g, r: (g, 0, 0)),
                pl.BlockSpec((LANES, LANES), lambda g, r: (0, 0)),
            ],
            out_specs=pl.BlockSpec((DEVICES, OUT_ROWS, LANES), lambda g, r: (0, 0, 0)),
            scratch_shapes=[
                pltpu.VMEM((2 * LANES, 2 * LANES), jnp.float32),
                pltpu.VMEM((2 * LANES, 2 * LANES), jnp.float32),
            ],
        ),
        out_shape=jax.ShapeDtypeStruct((DEVICES, OUT_ROWS, LANES), jnp.float32),
        compiler_params=pltpu.CompilerParams(vmem_limit_bytes=VMEM_LIMIT),
        cost_estimate=pl.CostEstimate(flops=2_500_000_000, bytes_accessed=10_000_000, transcendentals=0),
        name="mirror",
    )(rank, left, received, direct)


def body(cycle_inter, integrals):
    x = jnp.swapaxes(cycle_inter, 0, 1)
    v = jnp.swapaxes(integrals, 0, 1)
    rank = (lax.axis_index("row") * lax.axis_size("col") + lax.axis_index("col")).astype(jnp.int32).reshape(1)
    received = lax.all_to_all(pack(rank, x, v), AXES, 0, 0, tiled=True)
    left, direct = local(rank, x, v)
    parts = lax.all_to_all(mirror(rank, left, received, direct), AXES, 0, 0, tiled=True)
    return jnp.sum(parts, axis=0)


def solution(mesh):
    return jax.shard_map(
        body,
        mesh=mesh,
        in_specs=(P(None, AXES, None), P(None, AXES, None)),
        out_specs=P("row", None),
        check_vma=False,
    )
```

```python
import jax
import jax.numpy as jnp
from jax import lax
from jax.experimental import pallas as pl
from jax.experimental.pallas import tpu as pltpu
from jax.sharding import PartitionSpec as P

AXES = ("row", "col")
DEVICES = 128
WIDTH = 12
HALF = WIDTH // 2
BLOCK = WIDTH * HALF
LANES = 128
PACK_PEERS = 16
PACK_GROUPS = DEVICES // PACK_PEERS
PACK_ROWS = PACK_PEERS * WIDTH
PEERS = 32
GROUPS = DEVICES // PEERS
ROWS = PEERS * WIDTH
TERMS = PEERS * BLOCK
ROW_DEVICES = 16
COL_DEVICES = 8
OUT_ROWS = LANES // ROW_DEVICES
VMEM_LIMIT = 56 * 1024 * 1024


def split(value):
    high = value.astype(jnp.bfloat16)
    low = (value - high.astype(jnp.float32)).astype(jnp.bfloat16)
    return high, low


def dot(a, b):
    return lax.dot_general(a, b, (((1,), (0,)), ((), ())), preferred_element_type=jnp.float32)


def fold(acc):
    top = acc[:LANES, :LANES] + acc[:LANES, LANES:]
    return top + (acc[LANES:, :LANES] + acc[LANES:, LANES:])


def pack_kernel(rank_ref, x_ref, v_ref, out_ref, x_rows, v_rows, packed, x_sem, v_sem, out_sem):
    rank = rank_ref[0]
    own_group = rank // PACK_PEERS

    def x_copy(group):
        rows = pl.ds(group * PACK_ROWS, PACK_ROWS)
        return pltpu.make_async_copy(x_ref.at[pl.ds(0, HALF), rows], x_rows.at[group], x_sem.at[group])

    def v_copy(group):
        rows = pl.ds(group * PACK_ROWS, PACK_ROWS)
        return pltpu.make_async_copy(v_ref.at[:, rows], v_rows.at[group], v_sem.at[group])

    def pack_x(group, i):
        for c in range(HALF):
            rows = x_rows[group, c, pl.ds(WIDTH * i, WIDTH), :]
            packed[group * PACK_PEERS + i, pl.ds(WIDTH * c, WIDTH), :] = rows

    def pack_v(group, i):
        for d in range(WIDTH):
            rows = v_rows[group, d, pl.ds(WIDTH * i + HALF, HALF), :]
            packed[group * PACK_PEERS + i, pl.ds(HALF * d, HALF), :] = rows

    for group in range(PACK_GROUPS):

        @pl.when(group >= own_group)
        def _():
            x_copy(group).start()

        @pl.when(group <= own_group)
        def _():
            v_copy(group).start()

    def step(group, _):
        @pl.when(group >= own_group)
        def _():
            x_copy(group).wait()

        @pl.when(group <= own_group)
        def _():
            v_copy(group).wait()

        @pl.when(group > own_group)
        def _():
            for i in range(PACK_PEERS):
                pack_x(group, i)

        @pl.when(group < own_group)
        def _():
            for i in range(PACK_PEERS):
                pack_v(group, i)

        @pl.when(group == own_group)
        def _():
            for i in range(PACK_PEERS):
                below = group * PACK_PEERS + i < rank

                @pl.when(below)
                def _():
                    pack_v(group, i)

                @pl.when(jnp.logical_not(below))
                def _():
                    pack_x(group, i)

        peers = pl.ds(group * PACK_PEERS, PACK_PEERS)
        pltpu.make_async_copy(packed.at[peers], out_ref.at[peers], out_sem).start()
        return 0

    lax.fori_loop(0, PACK_GROUPS, step, 0)
    pltpu.make_async_copy(packed, out_ref, out_sem).wait()


def pack(rank, x, v):
    return pl.pallas_call(
        pack_kernel,
        in_specs=[
            pl.BlockSpec(memory_space=pltpu.SMEM),
            pl.BlockSpec(memory_space=pl.ANY),
            pl.BlockSpec(memory_space=pl.ANY),
        ],
        out_specs=pl.BlockSpec(memory_space=pl.ANY),
        out_shape=jax.ShapeDtypeStruct((DEVICES, BLOCK, LANES), jnp.float32),
        scratch_shapes=[
            pltpu.VMEM((PACK_GROUPS, HALF, PACK_ROWS, LANES), jnp.float32),
            pltpu.VMEM((PACK_GROUPS, WIDTH, PACK_ROWS, LANES), jnp.float32),
            pltpu.VMEM((DEVICES, BLOCK, LANES), jnp.float32),
            pltpu.SemaphoreType.DMA((PACK_GROUPS,)),
            pltpu.SemaphoreType.DMA((PACK_GROUPS,)),
            pltpu.SemaphoreType.DMA,
        ],
        compiler_params=pltpu.CompilerParams(vmem_limit_bytes=VMEM_LIMIT),
        cost_estimate=pl.CostEstimate(flops=0, bytes_accessed=12_000_000, transcendentals=0),
        name="pack",
    )(rank, x, v)


def local_kernel(rank_ref, x_ref, v_ref, left_ref, direct_ref, terms_ref, own_x_ref, own_v_ref, acc_ref):
    rank = rank_ref[0]
    group = pl.program_id(0)
    own_group = rank // PEERS

    @pl.when(group == 0)
    def _():
        acc_ref[...] = jnp.zeros_like(acc_ref)

    for i in range(PEERS):
        peer = group * PEERS + i

        @pl.when(peer > rank)
        def _():
            for c in range(HALF):
                terms_ref[pl.ds(BLOCK * i + c, WIDTH, stride=HALF), :] = x_ref[HALF + c, pl.ds(WIDTH * i, WIDTH), :]

        @pl.when(peer < rank)
        def _():
            for d in range(WIDTH):
                terms_ref[pl.ds(BLOCK * i + d, HALF, stride=WIDTH), :] = v_ref[d, pl.ds(WIDTH * i, HALF), :]

        @pl.when(peer == rank)
        def _():
            terms_ref[pl.ds(BLOCK * i, BLOCK), :] = jnp.zeros((BLOCK, LANES), jnp.float32)
            for c in range(WIDTH):
                own_x_ref[pl.ds(WIDTH * c, WIDTH), :] = x_ref[c, pl.ds(WIDTH * i, WIDTH), :]
                own_v_ref[pl.ds(c, WIDTH, stride=WIDTH), :] = v_ref[c, pl.ds(WIDTH * i, WIDTH), :]

    high, low = split(terms_ref[...].T)
    left_ref[0, :LANES, :] = high
    left_ref[0, LANES:, :] = low

    def add(x_rows, v_rows):
        left = jnp.concatenate(split(x_rows.T), axis=0)
        right = jnp.concatenate(split(v_rows), axis=1)
        acc_ref[...] += dot(left, right)

    @pl.when(group < own_group)
    def _():
        for d in range(WIDTH):
            add(x_ref[d], v_ref[d])

    @pl.when(group == own_group)
    def _():
        ids = group * ROWS + lax.broadcasted_iota(jnp.int32, (ROWS, LANES), 0)
        for d in range(WIDTH):
            add(x_ref[d], jnp.where(ids < rank * WIDTH + d, v_ref[d], 0.0))
        pair = lax.broadcasted_iota(jnp.int32, (WIDTH * WIDTH, LANES), 0)
        upper = pair % WIDTH > pair // WIDTH
        add(own_x_ref[...], jnp.where(upper, -own_v_ref[...], 0.0))

    @pl.when(group == GROUPS - 1)
    def _():
        direct_ref[...] = fold(acc_ref[...])


def local(rank, x, v):
    return pl.pallas_call(
        local_kernel,
        grid_spec=pltpu.PrefetchScalarGridSpec(
            num_scalar_prefetch=1,
            grid=(GROUPS,),
            in_specs=[
                pl.BlockSpec((WIDTH, ROWS, LANES), lambda g, r: (0, g, 0)),
                pl.BlockSpec((WIDTH, ROWS, LANES), lambda g, r: (0, jnp.minimum(g, r[0] // PEERS), 0)),
            ],
            out_specs=[
                pl.BlockSpec((1, 2 * LANES, TERMS), lambda g, r: (g, 0, 0)),
                pl.BlockSpec((LANES, LANES), lambda g, r: (0, 0)),
            ],
            scratch_shapes=[
                pltpu.VMEM((TERMS, LANES), jnp.float32),
                pltpu.VMEM((WIDTH * WIDTH, LANES), jnp.float32),
                pltpu.VMEM((WIDTH * WIDTH, LANES), jnp.float32),
                pltpu.VMEM((2 * LANES, 2 * LANES), jnp.float32),
            ],
        ),
        out_shape=[
            jax.ShapeDtypeStruct((GROUPS, 2 * LANES, TERMS), jnp.bfloat16),
            jax.ShapeDtypeStruct((LANES, LANES), jnp.float32),
        ],
        compiler_params=pltpu.CompilerParams(vmem_limit_bytes=VMEM_LIMIT),
        cost_estimate=pl.CostEstimate(flops=20_000_000_000, bytes_accessed=30_000_000, transcendentals=0),
        name="local",
    )(rank, x, v)


def mirror_kernel(
    rank_ref, left_ref, received_ref, direct_ref, out_ref, left, received, below_ref, above_ref, left_sem, received_sem
):
    rank = rank_ref[0]
    own_group = rank // PEERS

    def copies(turn):
        group = lax.rem(own_group + turn, GROUPS)
        peers = pl.ds(group * PEERS, PEERS)
        return (
            pltpu.make_async_copy(received_ref.at[peers], received.at[turn], received_sem.at[turn]),
            pltpu.make_async_copy(left_ref.at[group], left.at[turn], left_sem.at[turn]),
        )

    for turn in range(GROUPS):
        for copy in copies(turn):
            copy.start()

    def product(turn, values):
        return dot(left[turn], jnp.concatenate(split(values), axis=1))

    for copy in copies(0):
        copy.wait()
    values = received[0].reshape(TERMS, LANES)
    term = lax.broadcasted_iota(jnp.int32, (TERMS, LANES), 0)
    first = (rank - own_group * PEERS) * BLOCK
    below_ref[...] = product(0, jnp.where(term < first, values, 0.0))
    above_ref[...] = product(0, jnp.where(term >= first + BLOCK, values, 0.0))

    def step(turn, _):
        for copy in copies(turn):
            copy.wait()
        values = received[turn].reshape(TERMS, LANES)
        below = own_group + turn >= GROUPS

        @pl.when(below)
        def _():
            below_ref[...] += product(turn, values)

        @pl.when(jnp.logical_not(below))
        def _():
            above_ref[...] += product(turn, values)

        return 0

    lax.fori_loop(1, GROUPS, step, 0)
    total = direct_ref[...] - (fold(above_ref[...]) + fold(below_ref[...]).T)
    for row in range(ROW_DEVICES):
        rows = total[OUT_ROWS * row : OUT_ROWS * (row + 1), :]
        for col in range(COL_DEVICES):
            out_ref[COL_DEVICES * row + col] = rows


def mirror(rank, left, received, direct):
    return pl.pallas_call(
        mirror_kernel,
        in_specs=[
            pl.BlockSpec(memory_space=pltpu.SMEM),
            pl.BlockSpec(memory_space=pl.ANY),
            pl.BlockSpec(memory_space=pl.ANY),
            pl.BlockSpec(memory_space=pltpu.VMEM),
        ],
        out_specs=pl.BlockSpec(memory_space=pltpu.VMEM),
        out_shape=jax.ShapeDtypeStruct((DEVICES, OUT_ROWS, LANES), jnp.float32),
        scratch_shapes=[
            pltpu.VMEM((GROUPS, 2 * LANES, TERMS), jnp.bfloat16),
            pltpu.VMEM((GROUPS, PEERS, BLOCK, LANES), jnp.float32),
            pltpu.VMEM((2 * LANES, 2 * LANES), jnp.float32),
            pltpu.VMEM((2 * LANES, 2 * LANES), jnp.float32),
            pltpu.SemaphoreType.DMA((GROUPS,)),
            pltpu.SemaphoreType.DMA((GROUPS,)),
        ],
        compiler_params=pltpu.CompilerParams(vmem_limit_bytes=VMEM_LIMIT),
        cost_estimate=pl.CostEstimate(flops=2_500_000_000, bytes_accessed=10_000_000, transcendentals=0),
        name="mirror",
    )(rank, left, received, direct)


def body(cycle_inter, integrals):
    x = jnp.swapaxes(cycle_inter, 0, 1)
    v = jnp.swapaxes(integrals, 0, 1)
    rank = (lax.axis_index("row") * lax.axis_size("col") + lax.axis_index("col")).astype(jnp.int32).reshape(1)
    received = lax.all_to_all(pack(rank, x, v), AXES, 0, 0, tiled=True)
    left, direct = local(rank, x, v)
    parts = lax.all_to_all(mirror(rank, left, received, direct), AXES, 0, 0, tiled=True)
    return jnp.sum(parts, axis=0)


def solution(mesh):
    return jax.shard_map(
        body,
        mesh=mesh,
        in_specs=(P(None, AXES, None), P(None, AXES, None)),
        out_specs=P("row", None),
        check_vma=False,
    )
```

```python
import jax
import jax.numpy as jnp
from jax import lax
from jax.experimental import pallas as pl
from jax.experimental.pallas import tpu as pltpu
from jax.sharding import PartitionSpec as P

AXES = ("row", "col")
DEVICES = 128
WIDTH = 12
HALF = WIDTH // 2
BLOCK = WIDTH * HALF
LANES = 128
PACK_PEERS = 16
PACK_GROUPS = DEVICES // PACK_PEERS
PACK_ROWS = PACK_PEERS * WIDTH
PEERS = 32
GROUPS = DEVICES // PEERS
LEFT_GROUPS = 20
DIRECT_LENGTH = 320
ROWS = PEERS * WIDTH
TERMS = PEERS * BLOCK
ROW_DEVICES = 16
COL_DEVICES = 8
OUT_ROWS = LANES // ROW_DEVICES
VMEM_LIMIT = 56 * 1024 * 1024
MIRROR_VMEM_LIMIT = 44 * 1024 * 1024


def split(value):
    high = value.astype(jnp.bfloat16)
    low = (value - high.astype(jnp.float32)).astype(jnp.bfloat16)
    return high, low


def dot(a, b):
    return lax.dot_general(a, b, (((1,), (0,)), ((), ())), preferred_element_type=jnp.float32)


def fold(acc):
    top = acc[:LANES, :LANES] + acc[:LANES, LANES:]
    return top + (acc[LANES:, :LANES] + acc[LANES:, LANES:])


def pack_kernel(rank_ref, x_ref, v_ref, out_ref, rows_ref, own_ref, packed, in_sem, own_sem, out_sem):
    rank = rank_ref[0]
    own_group = rank // PACK_PEERS
    first, last, whole = pl.ds(0, HALF), pl.ds(HALF, HALF), pl.ds(0, WIDTH)

    def read(ref, columns, group):
        source = ref.at[columns, pl.ds(group * PACK_ROWS, PACK_ROWS)]
        return pltpu.make_async_copy(source, rows_ref.at[group, columns], in_sem.at[group])

    def read_own():
        source = v_ref.at[whole, pl.ds(own_group * PACK_ROWS, PACK_ROWS)]
        return pltpu.make_async_copy(source, own_ref, own_sem)

    def whole_rows(group, i, columns):
        for n, c in enumerate(columns):
            packed[group * PACK_PEERS + i, pl.ds(WIDTH * n, WIDTH), :] = rows_ref[group, c, pl.ds(WIDTH * i, WIDTH), :]

    def half_rows(group, i, start):
        for c in range(WIDTH):
            packed[group * PACK_PEERS + i, pl.ds(HALF * c, HALF), :] = rows_ref[
                group, c, pl.ds(WIDTH * i + start, HALF), :
            ]

    def cases(group):
        above = group > own_group
        below = group < own_group
        odd = lax.rem(group + own_group, 2) == 1
        even = jnp.logical_not(odd)
        return (
            (jnp.logical_and(above, even), x_ref, first, lambda i: whole_rows(group, i, range(HALF))),
            (jnp.logical_and(above, odd), x_ref, whole, lambda i: half_rows(group, i, 0)),
            (jnp.logical_and(below, odd), v_ref, last, lambda i: whole_rows(group, i, range(HALF, WIDTH))),
            (jnp.logical_and(below, even), v_ref, whole, lambda i: half_rows(group, i, HALF)),
        )

    read(x_ref, first, own_group).start()
    read_own().start()
    for group in range(PACK_GROUPS):
        for condition, ref, columns, _ in cases(group):

            @pl.when(condition)
            def _():
                read(ref, columns, group).start()

    def write(group):
        peers = pl.ds(group * PACK_PEERS, PACK_PEERS)
        pltpu.make_async_copy(packed.at[peers], out_ref.at[peers], out_sem).start()

    read(x_ref, first, own_group).wait()
    read_own().wait()
    for i in range(PACK_PEERS):
        below = own_group * PACK_PEERS + i < rank

        @pl.when(below)
        def _():
            for d in range(WIDTH):
                packed[own_group * PACK_PEERS + i, pl.ds(HALF * d, HALF), :] = own_ref[
                    d, pl.ds(WIDTH * i + HALF, HALF), :
                ]

        @pl.when(jnp.logical_not(below))
        def _():
            whole_rows(own_group, i, range(HALF))

    write(own_group)

    def step(group, _):
        for condition, ref, columns, move in cases(group):

            @pl.when(condition)
            def _():
                read(ref, columns, group).wait()
                for i in range(PACK_PEERS):
                    move(i)
                write(group)

        return 0

    lax.fori_loop(0, PACK_GROUPS, step, 0)
    pltpu.make_async_copy(packed, out_ref, out_sem).wait()


def pack(rank, x, v):
    return pl.pallas_call(
        pack_kernel,
        in_specs=[
            pl.BlockSpec(memory_space=pltpu.SMEM),
            pl.BlockSpec(memory_space=pl.ANY),
            pl.BlockSpec(memory_space=pl.ANY),
        ],
        out_specs=pl.BlockSpec(memory_space=pl.ANY),
        out_shape=jax.ShapeDtypeStruct((DEVICES, BLOCK, LANES), jnp.float32),
        scratch_shapes=[
            pltpu.VMEM((PACK_GROUPS, WIDTH, PACK_ROWS, LANES), jnp.float32),
            pltpu.VMEM((WIDTH, PACK_ROWS, LANES), jnp.float32),
            pltpu.VMEM((DEVICES, BLOCK, LANES), jnp.float32),
            pltpu.SemaphoreType.DMA((PACK_GROUPS,)),
            pltpu.SemaphoreType.DMA,
            pltpu.SemaphoreType.DMA,
        ],
        compiler_params=pltpu.CompilerParams(vmem_limit_bytes=VMEM_LIMIT),
        cost_estimate=pl.CostEstimate(flops=0, bytes_accessed=12_000_000, transcendentals=0),
        name="pack",
    )(rank, x, v)


def local_kernel(rank_ref, x_ref, v_ref, left_ref, direct_ref, terms_ref, own_x_ref, own_v_ref, acc_ref):
    rank = rank_ref[0]
    group = pl.program_id(0)
    own_group = rank // PEERS

    @pl.when(group == 0)
    def _():
        acc_ref[...] = jnp.zeros_like(acc_ref)

    own_pack_group = rank // PACK_PEERS
    for i in range(PEERS):
        peer = group * PEERS + i
        odd = lax.rem(group * (PEERS // PACK_PEERS) + i // PACK_PEERS + own_pack_group, 2) == 1
        even = jnp.logical_not(odd)
        above = peer > rank
        below = peer < rank

        @pl.when(jnp.logical_and(above, even))
        def _():
            for c in range(HALF):
                terms_ref[pl.ds(BLOCK * i + c, WIDTH, stride=HALF), :] = x_ref[HALF + c, pl.ds(WIDTH * i, WIDTH), :]

        @pl.when(jnp.logical_and(above, odd))
        def _():
            for c in range(WIDTH):
                terms_ref[pl.ds(BLOCK * i + c, HALF, stride=WIDTH), :] = x_ref[c, pl.ds(WIDTH * i + HALF, HALF), :]

        @pl.when(jnp.logical_and(below, even))
        def _():
            for d in range(WIDTH):
                terms_ref[pl.ds(BLOCK * i + d, HALF, stride=WIDTH), :] = v_ref[d, pl.ds(WIDTH * i, HALF), :]

        @pl.when(jnp.logical_and(below, odd))
        def _():
            for d in range(HALF):
                terms_ref[pl.ds(BLOCK * i + d, WIDTH, stride=HALF), :] = v_ref[d, pl.ds(WIDTH * i, WIDTH), :]

        @pl.when(peer == rank)
        def _():
            terms_ref[pl.ds(BLOCK * i, BLOCK), :] = jnp.zeros((BLOCK, LANES), jnp.float32)
            for c in range(WIDTH):
                own_x_ref[pl.ds(WIDTH * c, WIDTH), :] = x_ref[c, pl.ds(WIDTH * i, WIDTH), :]
                own_v_ref[pl.ds(c, WIDTH, stride=WIDTH), :] = v_ref[c, pl.ds(WIDTH * i, WIDTH), :]

    high, low = split(terms_ref[...].T)
    left_ref[0, :LANES, :] = high
    left_ref[0, LANES:, :] = low

    def add(x_rows, v_rows):
        left = jnp.concatenate(split(x_rows.T), axis=0)
        right = jnp.concatenate(split(v_rows), axis=1)
        acc_ref[...] += dot(left, right)

    @pl.when(group < own_group)
    def _():
        for d in range(WIDTH):
            add(x_ref[d], v_ref[d])

    @pl.when(group == own_group)
    def _():
        ids = group * ROWS + lax.broadcasted_iota(jnp.int32, (ROWS, LANES), 0)
        for d in range(WIDTH):
            add(x_ref[d], jnp.where(ids < rank * WIDTH + d, v_ref[d], 0.0))
        pair = lax.broadcasted_iota(jnp.int32, (WIDTH * WIDTH, LANES), 0)
        upper = pair % WIDTH > pair // WIDTH
        add(own_x_ref[...], jnp.where(upper, -own_v_ref[...], 0.0))

    @pl.when(group == GROUPS - 1)
    def _():
        direct_ref[0] = fold(acc_ref[...])


def local(rank, x, v):
    return pl.pallas_call(
        local_kernel,
        grid_spec=pltpu.PrefetchScalarGridSpec(
            num_scalar_prefetch=1,
            grid=(GROUPS,),
            in_specs=[
                pl.BlockSpec((WIDTH, ROWS, LANES), lambda g, r: (0, g, 0)),
                pl.BlockSpec((WIDTH, ROWS, LANES), lambda g, r: (0, jnp.minimum(g, r[0] // PEERS), 0)),
            ],
            out_specs=[
                pl.BlockSpec((1, 2 * LANES, TERMS), lambda g, r: (g, 0, 0)),
                pl.BlockSpec((1, LANES, LANES), lambda g, r: (0, 0, 0)),
            ],
            scratch_shapes=[
                pltpu.VMEM((TERMS, LANES), jnp.float32),
                pltpu.VMEM((WIDTH * WIDTH, LANES), jnp.float32),
                pltpu.VMEM((WIDTH * WIDTH, LANES), jnp.float32),
                pltpu.VMEM((2 * LANES, 2 * LANES), jnp.float32),
            ],
        ),
        out_shape=[
            jax.ShapeDtypeStruct((LEFT_GROUPS, 2 * LANES, TERMS), jnp.bfloat16),
            jax.ShapeDtypeStruct((DIRECT_LENGTH, LANES, LANES), jnp.float32),
        ],
        compiler_params=pltpu.CompilerParams(vmem_limit_bytes=VMEM_LIMIT),
        cost_estimate=pl.CostEstimate(flops=20_000_000_000, bytes_accessed=30_000_000, transcendentals=0),
        name="local",
    )(rank, x, v)


def mirror_kernel(
    rank_ref,
    left_ref,
    received_ref,
    direct_ref,
    out_ref,
    left,
    received,
    direct,
    below_ref,
    above_ref,
    left_sem,
    received_sem,
    direct_sem,
):
    rank = rank_ref[0]
    own_group = rank // PEERS

    def copies(turn):
        group = lax.rem(own_group + turn, GROUPS)
        peers = pl.ds(group * PEERS, PEERS)
        return (
            pltpu.make_async_copy(received_ref.at[peers], received.at[turn], received_sem.at[turn]),
            pltpu.make_async_copy(left_ref.at[group], left.at[turn], left_sem.at[turn]),
        )

    for turn in range(GROUPS):
        for copy in copies(turn):
            copy.start()
    direct_copy = pltpu.make_async_copy(direct_ref.at[0], direct, direct_sem)
    direct_copy.start()

    def product(turn, values):
        return dot(left[turn], jnp.concatenate(split(values), axis=1))

    for copy in copies(0):
        copy.wait()
    values = received[0].reshape(TERMS, LANES)
    term = lax.broadcasted_iota(jnp.int32, (TERMS, LANES), 0)
    first = (rank - own_group * PEERS) * BLOCK
    below_ref[...] = product(0, jnp.where(term < first, values, 0.0))
    above_ref[...] = product(0, jnp.where(term >= first + BLOCK, values, 0.0))

    def step(turn, _):
        for copy in copies(turn):
            copy.wait()
        values = received[turn].reshape(TERMS, LANES)
        below = own_group + turn >= GROUPS

        @pl.when(below)
        def _():
            below_ref[...] += product(turn, values)

        @pl.when(jnp.logical_not(below))
        def _():
            above_ref[...] += product(turn, values)

        return 0

    lax.fori_loop(1, GROUPS, step, 0)
    direct_copy.wait()
    total = direct[...] - (fold(above_ref[...]) + fold(below_ref[...]).T)
    for row in range(ROW_DEVICES):
        rows = total[OUT_ROWS * row : OUT_ROWS * (row + 1), :]
        for col in range(COL_DEVICES):
            out_ref[COL_DEVICES * row + col] = rows


def mirror(rank, left, received, direct):
    return pl.pallas_call(
        mirror_kernel,
        in_specs=[
            pl.BlockSpec(memory_space=pltpu.SMEM),
            pl.BlockSpec(memory_space=pl.ANY),
            pl.BlockSpec(memory_space=pl.ANY),
            pl.BlockSpec(memory_space=pl.ANY),
        ],
        out_specs=pl.BlockSpec(memory_space=pltpu.VMEM),
        out_shape=jax.ShapeDtypeStruct((DEVICES, OUT_ROWS, LANES), jnp.float32),
        scratch_shapes=[
            pltpu.VMEM((GROUPS, 2 * LANES, TERMS), jnp.bfloat16),
            pltpu.VMEM((GROUPS, PEERS, BLOCK, LANES), jnp.float32),
            pltpu.VMEM((LANES, LANES), jnp.float32),
            pltpu.VMEM((2 * LANES, 2 * LANES), jnp.float32),
            pltpu.VMEM((2 * LANES, 2 * LANES), jnp.float32),
            pltpu.SemaphoreType.DMA((GROUPS,)),
            pltpu.SemaphoreType.DMA((GROUPS,)),
            pltpu.SemaphoreType.DMA,
        ],
        compiler_params=pltpu.CompilerParams(vmem_limit_bytes=MIRROR_VMEM_LIMIT),
        cost_estimate=pl.CostEstimate(flops=2_500_000_000, bytes_accessed=10_000_000, transcendentals=0),
        name="mirror",
    )(rank, left, received, direct)


def body(cycle_inter, integrals):
    x = jnp.swapaxes(cycle_inter, 0, 1)
    v = jnp.swapaxes(integrals, 0, 1)
    rank = (lax.axis_index("row") * lax.axis_size("col") + lax.axis_index("col")).astype(jnp.int32).reshape(1)
    received = lax.all_to_all(pack(rank, x, v), AXES, 0, 0, tiled=True)
    left, direct = local(rank, x, v)
    parts = lax.all_to_all(mirror(rank, left, received, direct), AXES, 0, 0, tiled=True)
    return jnp.sum(parts, axis=0)


def solution(mesh):
    return jax.shard_map(
        body,
        mesh=mesh,
        in_specs=(P(None, AXES, None), P(None, AXES, None)),
        out_specs=P("row", None),
        check_vma=False,
    )
```

```python
import jax
import jax.numpy as jnp
from jax import lax
from jax.experimental import pallas as pl
from jax.experimental.pallas import tpu as pltpu
from jax.sharding import Mesh
from jax.sharding import PartitionSpec as P

AXES = ("half", "core", "col")
CHIPS = ("half", "col")
DEVICES = 128
WIDTH = 12
HALF = WIDTH // 2
BLOCK = WIDTH * HALF
LANES = 128
PACK_PEERS = 16
PACK_GROUPS = DEVICES // PACK_PEERS
PACK_ROWS = PACK_PEERS * WIDTH
PEERS = 32
GROUPS = DEVICES // PEERS
LEFT_GROUPS = 20
DIRECT_LENGTH = 320
ROWS = PEERS * WIDTH
TERMS = PEERS * BLOCK
CORES = 2
HALVES = 8
COL_DEVICES = 8
OUT_ROWS = LANES // (HALVES * CORES)
VMEM_LIMIT = 56 * 1024 * 1024
MIRROR_VMEM_LIMIT = 44 * 1024 * 1024


def split(value):
    high = value.astype(jnp.bfloat16)
    low = (value - high.astype(jnp.float32)).astype(jnp.bfloat16)
    return high, low


def dot(a, b):
    return lax.dot_general(a, b, (((1,), (0,)), ((), ())), preferred_element_type=jnp.float32)


def fold(acc):
    top = acc[:LANES, :LANES] + acc[:LANES, LANES:]
    return top + (acc[LANES:, :LANES] + acc[LANES:, LANES:])


def pack_kernel(rank_ref, x_ref, v_ref, out_ref, rows_ref, own_ref, packed, in_sem, own_sem, out_sem):
    rank = rank_ref[0]
    own_group = rank // PACK_PEERS
    first, last, whole = pl.ds(0, HALF), pl.ds(HALF, HALF), pl.ds(0, WIDTH)

    def read(ref, columns, group):
        source = ref.at[columns, pl.ds(group * PACK_ROWS, PACK_ROWS)]
        return pltpu.make_async_copy(source, rows_ref.at[group, columns], in_sem.at[group])

    def read_own():
        source = v_ref.at[whole, pl.ds(own_group * PACK_ROWS, PACK_ROWS)]
        return pltpu.make_async_copy(source, own_ref, own_sem)

    def whole_rows(group, i, columns):
        for n, c in enumerate(columns):
            packed[group * PACK_PEERS + i, pl.ds(WIDTH * n, WIDTH), :] = rows_ref[group, c, pl.ds(WIDTH * i, WIDTH), :]

    def half_rows(group, i, start):
        for c in range(WIDTH):
            packed[group * PACK_PEERS + i, pl.ds(HALF * c, HALF), :] = rows_ref[
                group, c, pl.ds(WIDTH * i + start, HALF), :
            ]

    def cases(group):
        above = group > own_group
        below = group < own_group
        odd = lax.rem(group + own_group, 2) == 1
        even = jnp.logical_not(odd)
        return (
            (jnp.logical_and(above, even), x_ref, first, lambda i: whole_rows(group, i, range(HALF))),
            (jnp.logical_and(above, odd), x_ref, whole, lambda i: half_rows(group, i, 0)),
            (jnp.logical_and(below, odd), v_ref, last, lambda i: whole_rows(group, i, range(HALF, WIDTH))),
            (jnp.logical_and(below, even), v_ref, whole, lambda i: half_rows(group, i, HALF)),
        )

    read(x_ref, first, own_group).start()
    read_own().start()
    for group in range(PACK_GROUPS):
        for condition, ref, columns, _ in cases(group):

            @pl.when(condition)
            def _():
                read(ref, columns, group).start()

    def write(group):
        peers = pl.ds(group * PACK_PEERS, PACK_PEERS)
        pltpu.make_async_copy(packed.at[peers], out_ref.at[peers], out_sem).start()

    read(x_ref, first, own_group).wait()
    read_own().wait()
    for i in range(PACK_PEERS):
        below = own_group * PACK_PEERS + i < rank

        @pl.when(below)
        def _():
            for d in range(WIDTH):
                packed[own_group * PACK_PEERS + i, pl.ds(HALF * d, HALF), :] = own_ref[
                    d, pl.ds(WIDTH * i + HALF, HALF), :
                ]

        @pl.when(jnp.logical_not(below))
        def _():
            whole_rows(own_group, i, range(HALF))

    write(own_group)

    def step(group, _):
        for condition, ref, columns, move in cases(group):

            @pl.when(condition)
            def _():
                read(ref, columns, group).wait()
                for i in range(PACK_PEERS):
                    move(i)
                write(group)

        return 0

    lax.fori_loop(0, PACK_GROUPS, step, 0)
    pltpu.make_async_copy(packed, out_ref, out_sem).wait()


def pack(rank, x, v):
    return pl.pallas_call(
        pack_kernel,
        in_specs=[
            pl.BlockSpec(memory_space=pltpu.SMEM),
            pl.BlockSpec(memory_space=pl.ANY),
            pl.BlockSpec(memory_space=pl.ANY),
        ],
        out_specs=pl.BlockSpec(memory_space=pl.ANY),
        out_shape=jax.ShapeDtypeStruct((DEVICES, BLOCK, LANES), jnp.float32),
        scratch_shapes=[
            pltpu.VMEM((PACK_GROUPS, WIDTH, PACK_ROWS, LANES), jnp.float32),
            pltpu.VMEM((WIDTH, PACK_ROWS, LANES), jnp.float32),
            pltpu.VMEM((DEVICES, BLOCK, LANES), jnp.float32),
            pltpu.SemaphoreType.DMA((PACK_GROUPS,)),
            pltpu.SemaphoreType.DMA,
            pltpu.SemaphoreType.DMA,
        ],
        compiler_params=pltpu.CompilerParams(vmem_limit_bytes=VMEM_LIMIT),
        cost_estimate=pl.CostEstimate(flops=0, bytes_accessed=12_000_000, transcendentals=0),
        name="pack",
    )(rank, x, v)


def local_kernel(rank_ref, x_ref, v_ref, left_ref, direct_ref, terms_ref, own_x_ref, own_v_ref, acc_ref):
    rank = rank_ref[0]
    group = pl.program_id(0)
    own_group = rank // PEERS

    @pl.when(group == 0)
    def _():
        acc_ref[...] = jnp.zeros_like(acc_ref)

    own_pack_group = rank // PACK_PEERS
    for i in range(PEERS):
        peer = group * PEERS + i
        odd = lax.rem(group * (PEERS // PACK_PEERS) + i // PACK_PEERS + own_pack_group, 2) == 1
        even = jnp.logical_not(odd)
        above = peer > rank
        below = peer < rank

        @pl.when(jnp.logical_and(above, even))
        def _():
            for c in range(HALF):
                terms_ref[pl.ds(BLOCK * i + c, WIDTH, stride=HALF), :] = x_ref[HALF + c, pl.ds(WIDTH * i, WIDTH), :]

        @pl.when(jnp.logical_and(above, odd))
        def _():
            for c in range(WIDTH):
                terms_ref[pl.ds(BLOCK * i + c, HALF, stride=WIDTH), :] = x_ref[c, pl.ds(WIDTH * i + HALF, HALF), :]

        @pl.when(jnp.logical_and(below, even))
        def _():
            for d in range(WIDTH):
                terms_ref[pl.ds(BLOCK * i + d, HALF, stride=WIDTH), :] = v_ref[d, pl.ds(WIDTH * i, HALF), :]

        @pl.when(jnp.logical_and(below, odd))
        def _():
            for d in range(HALF):
                terms_ref[pl.ds(BLOCK * i + d, WIDTH, stride=HALF), :] = v_ref[d, pl.ds(WIDTH * i, WIDTH), :]

        @pl.when(peer == rank)
        def _():
            terms_ref[pl.ds(BLOCK * i, BLOCK), :] = jnp.zeros((BLOCK, LANES), jnp.float32)
            for c in range(WIDTH):
                own_x_ref[pl.ds(WIDTH * c, WIDTH), :] = x_ref[c, pl.ds(WIDTH * i, WIDTH), :]
                own_v_ref[pl.ds(c, WIDTH, stride=WIDTH), :] = v_ref[c, pl.ds(WIDTH * i, WIDTH), :]

    high, low = split(terms_ref[...].T)
    left_ref[0, :LANES, :] = high
    left_ref[0, LANES:, :] = low

    def add(x_rows, v_rows):
        left = jnp.concatenate(split(x_rows.T), axis=0)
        right = jnp.concatenate(split(v_rows), axis=1)
        acc_ref[...] += dot(left, right)

    @pl.when(group < own_group)
    def _():
        for d in range(WIDTH):
            add(x_ref[d], v_ref[d])

    @pl.when(group == own_group)
    def _():
        ids = group * ROWS + lax.broadcasted_iota(jnp.int32, (ROWS, LANES), 0)
        for d in range(WIDTH):
            add(x_ref[d], jnp.where(ids < rank * WIDTH + d, v_ref[d], 0.0))
        pair = lax.broadcasted_iota(jnp.int32, (WIDTH * WIDTH, LANES), 0)
        upper = pair % WIDTH > pair // WIDTH
        add(own_x_ref[...], jnp.where(upper, -own_v_ref[...], 0.0))

    @pl.when(group == GROUPS - 1)
    def _():
        direct_ref[0] = fold(acc_ref[...])


def local(rank, x, v):
    return pl.pallas_call(
        local_kernel,
        grid_spec=pltpu.PrefetchScalarGridSpec(
            num_scalar_prefetch=1,
            grid=(GROUPS,),
            in_specs=[
                pl.BlockSpec((WIDTH, ROWS, LANES), lambda g, r: (0, g, 0)),
                pl.BlockSpec((WIDTH, ROWS, LANES), lambda g, r: (0, jnp.minimum(g, r[0] // PEERS), 0)),
            ],
            out_specs=[
                pl.BlockSpec((1, 2 * LANES, TERMS), lambda g, r: (g, 0, 0)),
                pl.BlockSpec((1, LANES, LANES), lambda g, r: (0, 0, 0)),
            ],
            scratch_shapes=[
                pltpu.VMEM((TERMS, LANES), jnp.float32),
                pltpu.VMEM((WIDTH * WIDTH, LANES), jnp.float32),
                pltpu.VMEM((WIDTH * WIDTH, LANES), jnp.float32),
                pltpu.VMEM((2 * LANES, 2 * LANES), jnp.float32),
            ],
        ),
        out_shape=[
            jax.ShapeDtypeStruct((LEFT_GROUPS, 2 * LANES, TERMS), jnp.bfloat16),
            jax.ShapeDtypeStruct((DIRECT_LENGTH, LANES, LANES), jnp.float32),
        ],
        compiler_params=pltpu.CompilerParams(vmem_limit_bytes=VMEM_LIMIT),
        cost_estimate=pl.CostEstimate(flops=20_000_000_000, bytes_accessed=30_000_000, transcendentals=0),
        name="local",
    )(rank, x, v)


def mirror_kernel(
    rank_ref,
    left_ref,
    received_ref,
    direct_ref,
    mine_ref,
    other_ref,
    left,
    received,
    direct,
    below_ref,
    above_ref,
    left_sem,
    received_sem,
    direct_sem,
):
    rank = rank_ref[0]
    own_group = rank // PEERS

    def copies(turn):
        group = lax.rem(own_group + turn, GROUPS)
        peers = pl.ds(group * PEERS, PEERS)
        return (
            pltpu.make_async_copy(received_ref.at[peers], received.at[turn], received_sem.at[turn]),
            pltpu.make_async_copy(left_ref.at[group], left.at[turn], left_sem.at[turn]),
        )

    for turn in range(GROUPS):
        for copy in copies(turn):
            copy.start()
    direct_copy = pltpu.make_async_copy(direct_ref.at[0], direct, direct_sem)
    direct_copy.start()

    def product(turn, values):
        return dot(left[turn], jnp.concatenate(split(values), axis=1))

    for copy in copies(0):
        copy.wait()
    values = received[0].reshape(TERMS, LANES)
    term = lax.broadcasted_iota(jnp.int32, (TERMS, LANES), 0)
    first = (rank - own_group * PEERS) * BLOCK
    below_ref[...] = product(0, jnp.where(term < first, values, 0.0))
    above_ref[...] = product(0, jnp.where(term >= first + BLOCK, values, 0.0))

    def step(turn, _):
        for copy in copies(turn):
            copy.wait()
        values = received[turn].reshape(TERMS, LANES)
        below = own_group + turn >= GROUPS

        @pl.when(below)
        def _():
            below_ref[...] += product(turn, values)

        @pl.when(jnp.logical_not(below))
        def _():
            above_ref[...] += product(turn, values)

        return 0

    lax.fori_loop(1, GROUPS, step, 0)
    direct_copy.wait()
    total = direct[...] - (fold(above_ref[...]) + fold(below_ref[...]).T)
    first_core = lax.rem(rank // COL_DEVICES, CORES) == 0
    for half in range(HALVES):
        start = half * CORES * OUT_ROWS
        zero = total[start : start + OUT_ROWS, :]
        one = total[start + OUT_ROWS : start + 2 * OUT_ROWS, :]
        mine_ref[half] = jnp.where(first_core, zero, one)
        other_ref[half] = jnp.where(first_core, one, zero)


def mirror(rank, left, received, direct):
    return pl.pallas_call(
        mirror_kernel,
        in_specs=[
            pl.BlockSpec(memory_space=pltpu.SMEM),
            pl.BlockSpec(memory_space=pl.ANY),
            pl.BlockSpec(memory_space=pl.ANY),
            pl.BlockSpec(memory_space=pl.ANY),
        ],
        out_specs=[pl.BlockSpec(memory_space=pltpu.VMEM)] * 2,
        out_shape=[jax.ShapeDtypeStruct((HALVES, OUT_ROWS, LANES), jnp.float32)] * 2,
        scratch_shapes=[
            pltpu.VMEM((GROUPS, 2 * LANES, TERMS), jnp.bfloat16),
            pltpu.VMEM((GROUPS, PEERS, BLOCK, LANES), jnp.float32),
            pltpu.VMEM((LANES, LANES), jnp.float32),
            pltpu.VMEM((2 * LANES, 2 * LANES), jnp.float32),
            pltpu.VMEM((2 * LANES, 2 * LANES), jnp.float32),
            pltpu.SemaphoreType.DMA((GROUPS,)),
            pltpu.SemaphoreType.DMA((GROUPS,)),
            pltpu.SemaphoreType.DMA,
        ],
        compiler_params=pltpu.CompilerParams(vmem_limit_bytes=MIRROR_VMEM_LIMIT),
        cost_estimate=pl.CostEstimate(flops=2_500_000_000, bytes_accessed=10_000_000, transcendentals=0),
        name="mirror",
    )(rank, left, received, direct)


def body(cycle_inter, integrals):
    x = jnp.swapaxes(cycle_inter, 0, 1)
    v = jnp.swapaxes(integrals, 0, 1)
    rank = lax.axis_index(AXES).astype(jnp.int32).reshape(1)
    received = lax.all_to_all(pack(rank, x, v), AXES, 0, 0, tiled=True)
    left, direct = local(rank, x, v)
    mine, other = mirror(rank, left, received, direct)
    rows = mine + lax.ppermute(other, "core", [(0, 1), (1, 0)])
    parts = jnp.broadcast_to(rows[:, None], (HALVES, COL_DEVICES, OUT_ROWS, LANES))
    parts = parts.reshape(HALVES * COL_DEVICES, OUT_ROWS, LANES)
    return jnp.sum(lax.all_to_all(parts, CHIPS, 0, 0, tiled=True), axis=0)


def solution(mesh):
    cores = Mesh(mesh.devices.reshape(HALVES, CORES, COL_DEVICES), AXES)
    return jax.shard_map(
        body,
        mesh=cores,
        in_specs=(P(None, AXES, None), P(None, AXES, None)),
        out_specs=P(("half", "core"), None),
        check_vma=False,
    )
```

```python
import jax
import jax.numpy as jnp
from jax import lax
from jax.experimental import pallas as pl
from jax.experimental.pallas import tpu as pltpu
from jax.sharding import Mesh
from jax.sharding import PartitionSpec as P

AXES = ("half", "core", "col")
CHIPS = ("half", "col")
DEVICES = 128
WIDTH = 12
HALF = WIDTH // 2
BLOCK = WIDTH * HALF
LANES = 128
PACK_PEERS = 16
PACK_GROUPS = DEVICES // PACK_PEERS
PACK_PAIRS = PACK_PEERS // 2
PAIR_ROWS = 2 * WIDTH
TILE = 8
PEERS = 32
GROUPS = DEVICES // PEERS
LEFT_GROUPS = 20
DIRECT_LENGTH = 320
ROWS = PEERS * WIDTH
TERMS = PEERS * BLOCK
CORES = 2
HALVES = 8
COL_DEVICES = 8
OUT_ROWS = LANES // (HALVES * CORES)
VMEM_LIMIT = 56 * 1024 * 1024
MIRROR_VMEM_LIMIT = 44 * 1024 * 1024


def split(value):
    high = value.astype(jnp.bfloat16)
    low = (value - high.astype(jnp.float32)).astype(jnp.bfloat16)
    return high, low


def dot(a, b):
    return lax.dot_general(a, b, (((1,), (0,)), ((), ())), preferred_element_type=jnp.float32)


def fold(acc):
    top = acc[:LANES, :LANES] + acc[:LANES, LANES:]
    return top + (acc[LANES:, :LANES] + acc[LANES:, LANES:])


def pack_kernel(rank_ref, x_ref, v_ref, out_ref, rows_ref, own_ref, packed, in_sem, own_sem, out_sem):
    rank = rank_ref[0]
    own_group = rank // PACK_PEERS
    own_half = HALF * (1 - lax.rem(rank, 2))

    def whole_copies(ref, group):
        columns = pl.ds(own_half, HALF)
        source = ref.at[columns, pl.ds(group * PACK_PAIRS, PACK_PAIRS)]
        return (pltpu.make_async_copy(source, rows_ref.at[group, pl.ds(0, HALF)], in_sem.at[group, 0]),)

    def outer_copies(ref, group, target, sems):
        pairs = pl.ds(group * PACK_PAIRS, PACK_PAIRS)
        return tuple(
            pltpu.make_async_copy(
                ref.at[:, pairs, pl.ds(start, TILE)], target.at[:, :, pl.ds(start, TILE)], sems.at[n]
            )
            for n, start in enumerate((0, PAIR_ROWS - TILE))
        )

    def half_copies(ref, group):
        return outer_copies(ref, group, rows_ref.at[group], in_sem.at[group])

    def own_copies():
        return outer_copies(v_ref, own_group, own_ref, own_sem)

    def whole_rows(group, i):
        for n in range(HALF):
            rows = rows_ref[group, n, i // 2, pl.ds(WIDTH * (i % 2), WIDTH), :]
            packed[group * PACK_PEERS + i, pl.ds(WIDTH * n, WIDTH), :] = rows

    def half_start(i):
        return (WIDTH + HALF) * (i % 2)

    def half_rows(group, i):
        for c in range(WIDTH):
            rows = rows_ref[group, c, i // 2, pl.ds(half_start(i), HALF), :]
            packed[group * PACK_PEERS + i, pl.ds(HALF * c, HALF), :] = rows

    def cases(group):
        above = group > own_group
        below = group < own_group
        odd = lax.rem(group + own_group, 2) == 1
        even = jnp.logical_not(odd)
        return (
            (jnp.logical_and(above, even), x_ref, whole_copies, whole_rows),
            (jnp.logical_and(above, odd), x_ref, half_copies, half_rows),
            (jnp.logical_and(below, odd), v_ref, whole_copies, whole_rows),
            (jnp.logical_and(below, even), v_ref, half_copies, half_rows),
        )

    for copy in whole_copies(x_ref, own_group) + own_copies():
        copy.start()
    for group in range(PACK_GROUPS):
        for condition, ref, copies, _ in cases(group):

            @pl.when(condition)
            def _():
                for copy in copies(ref, group):
                    copy.start()

    def write(group):
        peers = pl.ds(group * PACK_PEERS, PACK_PEERS)
        pltpu.make_async_copy(packed.at[peers], out_ref.at[peers], out_sem).start()

    for copy in whole_copies(x_ref, own_group) + own_copies():
        copy.wait()
    for i in range(PACK_PEERS):
        below = own_group * PACK_PEERS + i < rank

        @pl.when(below)
        def _():
            for d in range(WIDTH):
                rows = own_ref[d, i // 2, pl.ds(half_start(i), HALF), :]
                packed[own_group * PACK_PEERS + i, pl.ds(HALF * d, HALF), :] = rows

        @pl.when(jnp.logical_not(below))
        def _():
            whole_rows(own_group, i)

    write(own_group)

    def step(group, _):
        for condition, ref, copies, move in cases(group):

            @pl.when(condition)
            def _():
                for copy in copies(ref, group):
                    copy.wait()
                for i in range(PACK_PEERS):
                    move(group, i)
                write(group)

        return 0

    lax.fori_loop(0, PACK_GROUPS, step, 0)
    pltpu.make_async_copy(packed, out_ref, out_sem).wait()


def pack(rank, x, v):
    x, v = (array.reshape(WIDTH, DEVICES // 2, PAIR_ROWS, LANES) for array in (x, v))
    return pl.pallas_call(
        pack_kernel,
        in_specs=[
            pl.BlockSpec(memory_space=pltpu.SMEM),
            pl.BlockSpec(memory_space=pl.ANY),
            pl.BlockSpec(memory_space=pl.ANY),
        ],
        out_specs=pl.BlockSpec(memory_space=pl.ANY),
        out_shape=jax.ShapeDtypeStruct((DEVICES, BLOCK, LANES), jnp.float32),
        scratch_shapes=[
            pltpu.VMEM((PACK_GROUPS, WIDTH, PACK_PAIRS, PAIR_ROWS, LANES), jnp.float32),
            pltpu.VMEM((WIDTH, PACK_PAIRS, PAIR_ROWS, LANES), jnp.float32),
            pltpu.VMEM((DEVICES, BLOCK, LANES), jnp.float32),
            pltpu.SemaphoreType.DMA((PACK_GROUPS, 2)),
            pltpu.SemaphoreType.DMA((2,)),
            pltpu.SemaphoreType.DMA,
        ],
        compiler_params=pltpu.CompilerParams(vmem_limit_bytes=VMEM_LIMIT),
        cost_estimate=pl.CostEstimate(flops=0, bytes_accessed=12_000_000, transcendentals=0),
        name="pack",
    )(rank, x, v)


def local_kernel(rank_ref, x_ref, v_ref, left_ref, direct_ref, terms_ref, own_x_ref, own_v_ref, acc_ref):
    rank = rank_ref[0]
    group = pl.program_id(0)
    own_group = rank // PEERS

    @pl.when(group == 0)
    def _():
        acc_ref[...] = jnp.zeros_like(acc_ref)

    own_pack_group = rank // PACK_PEERS
    own_half = HALF * lax.rem(rank, 2)
    for i in range(PEERS):
        peer = group * PEERS + i
        odd = lax.rem(group * (PEERS // PACK_PEERS) + i // PACK_PEERS + own_pack_group, 2) == 1
        even = jnp.logical_not(odd)
        above = peer > rank
        below = peer < rank

        def from_whole(ref):
            start = WIDTH * i + HALF * (1 - i % 2)
            for m in range(WIDTH):
                terms_ref[pl.ds(BLOCK * i + m, HALF, stride=WIDTH), :] = ref[m, pl.ds(start, HALF), :]

        def from_half(ref):
            for m in range(HALF):
                rows = ref[own_half + m, pl.ds(WIDTH * i, WIDTH), :]
                terms_ref[pl.ds(BLOCK * i + m, WIDTH, stride=HALF), :] = rows

        @pl.when(jnp.logical_and(above, even))
        def _():
            from_half(x_ref)

        @pl.when(jnp.logical_and(above, odd))
        def _():
            from_whole(x_ref)

        @pl.when(jnp.logical_and(below, even))
        def _():
            from_whole(v_ref)

        @pl.when(jnp.logical_and(below, odd))
        def _():
            from_half(v_ref)

        @pl.when(peer == rank)
        def _():
            terms_ref[pl.ds(BLOCK * i, BLOCK), :] = jnp.zeros((BLOCK, LANES), jnp.float32)
            for c in range(WIDTH):
                own_x_ref[pl.ds(WIDTH * c, WIDTH), :] = x_ref[c, pl.ds(WIDTH * i, WIDTH), :]
                own_v_ref[pl.ds(c, WIDTH, stride=WIDTH), :] = v_ref[c, pl.ds(WIDTH * i, WIDTH), :]

    high, low = split(terms_ref[...].T)
    left_ref[0, :LANES, :] = high
    left_ref[0, LANES:, :] = low

    def add(x_rows, v_rows):
        left = jnp.concatenate(split(x_rows.T), axis=0)
        right = jnp.concatenate(split(v_rows), axis=1)
        acc_ref[...] += dot(left, right)

    @pl.when(group < own_group)
    def _():
        for d in range(WIDTH):
            add(x_ref[d], v_ref[d])

    @pl.when(group == own_group)
    def _():
        ids = group * ROWS + lax.broadcasted_iota(jnp.int32, (ROWS, LANES), 0)
        for d in range(WIDTH):
            add(x_ref[d], jnp.where(ids < rank * WIDTH + d, v_ref[d], 0.0))
        pair = lax.broadcasted_iota(jnp.int32, (WIDTH * WIDTH, LANES), 0)
        upper = pair % WIDTH > pair // WIDTH
        add(own_x_ref[...], jnp.where(upper, -own_v_ref[...], 0.0))

    @pl.when(group == GROUPS - 1)
    def _():
        direct_ref[0] = fold(acc_ref[...])


def local(rank, x, v):
    return pl.pallas_call(
        local_kernel,
        grid_spec=pltpu.PrefetchScalarGridSpec(
            num_scalar_prefetch=1,
            grid=(GROUPS,),
            in_specs=[
                pl.BlockSpec((WIDTH, ROWS, LANES), lambda g, r: (0, g, 0)),
                pl.BlockSpec((WIDTH, ROWS, LANES), lambda g, r: (0, jnp.minimum(g, r[0] // PEERS), 0)),
            ],
            out_specs=[
                pl.BlockSpec((1, 2 * LANES, TERMS), lambda g, r: (g, 0, 0)),
                pl.BlockSpec((1, LANES, LANES), lambda g, r: (0, 0, 0)),
            ],
            scratch_shapes=[
                pltpu.VMEM((TERMS, LANES), jnp.float32),
                pltpu.VMEM((WIDTH * WIDTH, LANES), jnp.float32),
                pltpu.VMEM((WIDTH * WIDTH, LANES), jnp.float32),
                pltpu.VMEM((2 * LANES, 2 * LANES), jnp.float32),
            ],
        ),
        out_shape=[
            jax.ShapeDtypeStruct((LEFT_GROUPS, 2 * LANES, TERMS), jnp.bfloat16),
            jax.ShapeDtypeStruct((DIRECT_LENGTH, LANES, LANES), jnp.float32),
        ],
        compiler_params=pltpu.CompilerParams(vmem_limit_bytes=VMEM_LIMIT),
        cost_estimate=pl.CostEstimate(flops=20_000_000_000, bytes_accessed=30_000_000, transcendentals=0),
        name="local",
    )(rank, x, v)


def mirror_kernel(
    rank_ref,
    left_ref,
    received_ref,
    direct_ref,
    mine_ref,
    other_ref,
    left,
    received,
    direct,
    below_ref,
    above_ref,
    left_sem,
    received_sem,
    direct_sem,
):
    rank = rank_ref[0]
    own_group = rank // PEERS

    def copies(turn):
        group = lax.rem(own_group + turn, GROUPS)
        peers = pl.ds(group * PEERS, PEERS)
        return (
            pltpu.make_async_copy(received_ref.at[peers], received.at[turn], received_sem.at[turn]),
            pltpu.make_async_copy(left_ref.at[group], left.at[turn], left_sem.at[turn]),
        )

    for turn in range(GROUPS):
        for copy in copies(turn):
            copy.start()
    direct_copy = pltpu.make_async_copy(direct_ref.at[0], direct, direct_sem)
    direct_copy.start()

    def product(turn, values):
        return dot(left[turn], jnp.concatenate(split(values), axis=1))

    for copy in copies(0):
        copy.wait()
    values = received[0].reshape(TERMS, LANES)
    term = lax.broadcasted_iota(jnp.int32, (TERMS, LANES), 0)
    first = (rank - own_group * PEERS) * BLOCK
    below_ref[...] = product(0, jnp.where(term < first, values, 0.0))
    above_ref[...] = product(0, jnp.where(term >= first + BLOCK, values, 0.0))

    def step(turn, _):
        for copy in copies(turn):
            copy.wait()
        values = received[turn].reshape(TERMS, LANES)
        below = own_group + turn >= GROUPS

        @pl.when(below)
        def _():
            below_ref[...] += product(turn, values)

        @pl.when(jnp.logical_not(below))
        def _():
            above_ref[...] += product(turn, values)

        return 0

    lax.fori_loop(1, GROUPS, step, 0)
    direct_copy.wait()
    total = direct[...] - (fold(above_ref[...]) + fold(below_ref[...]).T)
    first_core = lax.rem(rank // COL_DEVICES, CORES) == 0
    for half in range(HALVES):
        start = half * CORES * OUT_ROWS
        zero = total[start : start + OUT_ROWS, :]
        one = total[start + OUT_ROWS : start + 2 * OUT_ROWS, :]
        mine_ref[half] = jnp.where(first_core, zero, one)
        other_ref[half] = jnp.where(first_core, one, zero)


def mirror(rank, left, received, direct):
    return pl.pallas_call(
        mirror_kernel,
        in_specs=[
            pl.BlockSpec(memory_space=pltpu.SMEM),
            pl.BlockSpec(memory_space=pl.ANY),
            pl.BlockSpec(memory_space=pl.ANY),
            pl.BlockSpec(memory_space=pl.ANY),
        ],
        out_specs=[pl.BlockSpec(memory_space=pltpu.VMEM)] * 2,
        out_shape=[jax.ShapeDtypeStruct((HALVES, OUT_ROWS, LANES), jnp.float32)] * 2,
        scratch_shapes=[
            pltpu.VMEM((GROUPS, 2 * LANES, TERMS), jnp.bfloat16),
            pltpu.VMEM((GROUPS, PEERS, BLOCK, LANES), jnp.float32),
            pltpu.VMEM((LANES, LANES), jnp.float32),
            pltpu.VMEM((2 * LANES, 2 * LANES), jnp.float32),
            pltpu.VMEM((2 * LANES, 2 * LANES), jnp.float32),
            pltpu.SemaphoreType.DMA((GROUPS,)),
            pltpu.SemaphoreType.DMA((GROUPS,)),
            pltpu.SemaphoreType.DMA,
        ],
        compiler_params=pltpu.CompilerParams(vmem_limit_bytes=MIRROR_VMEM_LIMIT),
        cost_estimate=pl.CostEstimate(flops=2_500_000_000, bytes_accessed=10_000_000, transcendentals=0),
        name="mirror",
    )(rank, left, received, direct)


def body(cycle_inter, integrals):
    x = jnp.swapaxes(cycle_inter, 0, 1)
    v = jnp.swapaxes(integrals, 0, 1)
    rank = lax.axis_index(AXES).astype(jnp.int32).reshape(1)
    received = lax.all_to_all(pack(rank, x, v), AXES, 0, 0, tiled=True)
    left, direct = local(rank, x, v)
    mine, other = mirror(rank, left, received, direct)
    rows = mine + lax.ppermute(other, "core", [(0, 1), (1, 0)])
    parts = jnp.broadcast_to(rows[:, None], (HALVES, COL_DEVICES, OUT_ROWS, LANES))
    parts = parts.reshape(HALVES * COL_DEVICES, OUT_ROWS, LANES)
    return jnp.sum(lax.all_to_all(parts, CHIPS, 0, 0, tiled=True), axis=0)


def solution(mesh):
    cores = Mesh(mesh.devices.reshape(HALVES, CORES, COL_DEVICES), AXES)
    return jax.shard_map(
        body,
        mesh=cores,
        in_specs=(P(None, AXES, None), P(None, AXES, None)),
        out_specs=P(("half", "core"), None),
        check_vma=False,
    )
```

```python
import jax
import jax.numpy as jnp
from jax import lax
from jax.experimental import pallas as pl
from jax.experimental.pallas import tpu as pltpu
from jax.sharding import Mesh
from jax.sharding import PartitionSpec as P

AXES = ("half", "core", "col")
CHIPS = ("half", "col")
DEVICES = 128
WIDTH = 12
HALF = WIDTH // 2
BLOCK = WIDTH * HALF
LANES = 128
PACK_PEERS = 16
PACK_GROUPS = DEVICES // PACK_PEERS
PACK_PAIRS = PACK_PEERS // 2
PAIR_ROWS = 2 * WIDTH
TILE = 8
PEERS = 32
GROUPS = DEVICES // PEERS
LEFT_GROUPS = 20
DIRECT_LENGTH = 320
ROWS = PEERS * WIDTH
TERMS = PEERS * BLOCK
CORES = 2
HALVES = 8
COL_DEVICES = 8
OUT_ROWS = LANES // (HALVES * CORES)
VMEM_LIMIT = 56 * 1024 * 1024
MIRROR_VMEM_LIMIT = 44 * 1024 * 1024


def split(value):
    high = value.astype(jnp.bfloat16)
    low = (value - high.astype(jnp.float32)).astype(jnp.bfloat16)
    return high, low


def dot(a, b):
    return lax.dot_general(a, b, (((1,), (0,)), ((), ())), preferred_element_type=jnp.float32)


def fold(acc):
    top = acc[:LANES, :LANES] + acc[:LANES, LANES:]
    return top + (acc[LANES:, :LANES] + acc[LANES:, LANES:])


def pack_kernel(rank_ref, x_ref, v_ref, out_ref, rows_ref, own_ref, packed, in_sem, own_sem, out_sem):
    rank = rank_ref[0]
    own_group = rank // PACK_PEERS
    own_half = HALF * (1 - lax.rem(rank, 2))

    def v_copies(group, target, sem):
        source = v_ref.at[pl.ds(own_half, HALF), pl.ds(group * PACK_PAIRS, PACK_PAIRS)]
        return (pltpu.make_async_copy(source, target, sem),)

    def x_copies(group):
        pairs = pl.ds(group * PACK_PAIRS, PACK_PAIRS)
        return tuple(
            pltpu.make_async_copy(
                x_ref.at[:, pairs, pl.ds(start, TILE)], rows_ref.at[group, :, :, pl.ds(start, TILE)], in_sem.at[group, n]
            )
            for n, start in enumerate((0, PAIR_ROWS - TILE))
        )

    def below_copies(group):
        return v_copies(group, rows_ref.at[group, pl.ds(0, HALF)], in_sem.at[group, 0])

    def own_copies():
        return x_copies(own_group) + v_copies(own_group, own_ref, own_sem)

    def pack_v(group, i, source):
        for n in range(HALF):
            rows = source[n, i // 2, pl.ds(WIDTH * (i % 2), WIDTH), :]
            packed[group * PACK_PEERS + i, pl.ds(WIDTH * n, WIDTH), :] = rows

    def pack_x(group, i):
        for c in range(WIDTH):
            rows = rows_ref[group, c, i // 2, pl.ds((WIDTH + HALF) * (i % 2), HALF), :]
            packed[group * PACK_PEERS + i, pl.ds(HALF * c, HALF), :] = rows

    for copy in own_copies():
        copy.start()
    for group in range(PACK_GROUPS):

        @pl.when(group > own_group)
        def _():
            for copy in x_copies(group):
                copy.start()

        @pl.when(group < own_group)
        def _():
            for copy in below_copies(group):
                copy.start()

    def write(group):
        peers = pl.ds(group * PACK_PEERS, PACK_PEERS)
        pltpu.make_async_copy(packed.at[peers], out_ref.at[peers], out_sem).start()

    for copy in own_copies():
        copy.wait()
    for i in range(PACK_PEERS):
        below = own_group * PACK_PEERS + i < rank

        @pl.when(below)
        def _():
            pack_v(own_group, i, own_ref)

        @pl.when(jnp.logical_not(below))
        def _():
            pack_x(own_group, i)

    write(own_group)

    def step(group, _):
        @pl.when(group > own_group)
        def _():
            for copy in x_copies(group):
                copy.wait()
            for i in range(PACK_PEERS):
                pack_x(group, i)
            write(group)

        @pl.when(group < own_group)
        def _():
            for copy in below_copies(group):
                copy.wait()
            for i in range(PACK_PEERS):
                pack_v(group, i, rows_ref.at[group])
            write(group)

        return 0

    lax.fori_loop(0, PACK_GROUPS, step, 0)
    pltpu.make_async_copy(packed, out_ref, out_sem).wait()


def pack(rank, x, v):
    x, v = (array.reshape(WIDTH, DEVICES // 2, PAIR_ROWS, LANES) for array in (x, v))
    return pl.pallas_call(
        pack_kernel,
        in_specs=[
            pl.BlockSpec(memory_space=pltpu.SMEM),
            pl.BlockSpec(memory_space=pl.ANY),
            pl.BlockSpec(memory_space=pl.ANY),
        ],
        out_specs=pl.BlockSpec(memory_space=pl.ANY),
        out_shape=jax.ShapeDtypeStruct((DEVICES, BLOCK, LANES), jnp.float32),
        scratch_shapes=[
            pltpu.VMEM((PACK_GROUPS, WIDTH, PACK_PAIRS, PAIR_ROWS, LANES), jnp.float32),
            pltpu.VMEM((HALF, PACK_PAIRS, PAIR_ROWS, LANES), jnp.float32),
            pltpu.VMEM((DEVICES, BLOCK, LANES), jnp.float32),
            pltpu.SemaphoreType.DMA((PACK_GROUPS, 2)),
            pltpu.SemaphoreType.DMA,
            pltpu.SemaphoreType.DMA,
        ],
        compiler_params=pltpu.CompilerParams(vmem_limit_bytes=VMEM_LIMIT),
        cost_estimate=pl.CostEstimate(flops=0, bytes_accessed=12_000_000, transcendentals=0),
        name="pack",
    )(rank, x, v)


def local_kernel(rank_ref, x_ref, v_ref, left_ref, direct_ref, terms_ref, own_x_ref, own_v_ref, acc_ref):
    rank = rank_ref[0]
    group = pl.program_id(0)
    own_group = rank // PEERS

    @pl.when(group == 0)
    def _():
        acc_ref[...] = jnp.zeros_like(acc_ref)

    own_half = HALF * lax.rem(rank, 2)
    for i in range(PEERS):
        peer = group * PEERS + i

        @pl.when(peer > rank)
        def _():
            start = WIDTH * i + HALF * (1 - i % 2)
            for m in range(WIDTH):
                terms_ref[pl.ds(BLOCK * i + m, HALF, stride=WIDTH), :] = x_ref[m, pl.ds(start, HALF), :]

        @pl.when(peer < rank)
        def _():
            for m in range(HALF):
                rows = v_ref[own_half + m, pl.ds(WIDTH * i, WIDTH), :]
                terms_ref[pl.ds(BLOCK * i + m, WIDTH, stride=HALF), :] = rows

        @pl.when(peer == rank)
        def _():
            terms_ref[pl.ds(BLOCK * i, BLOCK), :] = jnp.zeros((BLOCK, LANES), jnp.float32)
            for c in range(WIDTH):
                own_x_ref[pl.ds(WIDTH * c, WIDTH), :] = x_ref[c, pl.ds(WIDTH * i, WIDTH), :]
                own_v_ref[pl.ds(c, WIDTH, stride=WIDTH), :] = v_ref[c, pl.ds(WIDTH * i, WIDTH), :]

    high, low = split(terms_ref[...].T)
    left_ref[0, :LANES, :] = high
    left_ref[0, LANES:, :] = low

    def add(x_rows, v_rows):
        left = jnp.concatenate(split(x_rows.T), axis=0)
        right = jnp.concatenate(split(v_rows), axis=1)
        acc_ref[...] += dot(left, right)

    @pl.when(group < own_group)
    def _():
        for d in range(WIDTH):
            add(x_ref[d], v_ref[d])

    @pl.when(group == own_group)
    def _():
        ids = group * ROWS + lax.broadcasted_iota(jnp.int32, (ROWS, LANES), 0)
        for d in range(WIDTH):
            add(x_ref[d], jnp.where(ids < rank * WIDTH + d, v_ref[d], 0.0))
        pair = lax.broadcasted_iota(jnp.int32, (WIDTH * WIDTH, LANES), 0)
        upper = pair % WIDTH > pair // WIDTH
        add(own_x_ref[...], jnp.where(upper, -own_v_ref[...], 0.0))

    @pl.when(group == GROUPS - 1)
    def _():
        direct_ref[0] = fold(acc_ref[...])


def local(rank, x, v):
    return pl.pallas_call(
        local_kernel,
        grid_spec=pltpu.PrefetchScalarGridSpec(
            num_scalar_prefetch=1,
            grid=(GROUPS,),
            in_specs=[
                pl.BlockSpec((WIDTH, ROWS, LANES), lambda g, r: (0, g, 0)),
                pl.BlockSpec((WIDTH, ROWS, LANES), lambda g, r: (0, jnp.minimum(g, r[0] // PEERS), 0)),
            ],
            out_specs=[
                pl.BlockSpec((1, 2 * LANES, TERMS), lambda g, r: (g, 0, 0)),
                pl.BlockSpec((1, LANES, LANES), lambda g, r: (0, 0, 0)),
            ],
            scratch_shapes=[
                pltpu.VMEM((TERMS, LANES), jnp.float32),
                pltpu.VMEM((WIDTH * WIDTH, LANES), jnp.float32),
                pltpu.VMEM((WIDTH * WIDTH, LANES), jnp.float32),
                pltpu.VMEM((2 * LANES, 2 * LANES), jnp.float32),
            ],
        ),
        out_shape=[
            jax.ShapeDtypeStruct((LEFT_GROUPS, 2 * LANES, TERMS), jnp.bfloat16),
            jax.ShapeDtypeStruct((DIRECT_LENGTH, LANES, LANES), jnp.float32),
        ],
        compiler_params=pltpu.CompilerParams(vmem_limit_bytes=VMEM_LIMIT),
        cost_estimate=pl.CostEstimate(flops=20_000_000_000, bytes_accessed=30_000_000, transcendentals=0),
        name="local",
    )(rank, x, v)


def mirror_kernel(
    rank_ref,
    left_ref,
    received_ref,
    direct_ref,
    mine_ref,
    other_ref,
    left,
    received,
    direct,
    below_ref,
    above_ref,
    left_sem,
    received_sem,
    direct_sem,
):
    rank = rank_ref[0]
    own_group = rank // PEERS

    def copies(turn):
        group = lax.rem(own_group + turn, GROUPS)
        peers = pl.ds(group * PEERS, PEERS)
        return (
            pltpu.make_async_copy(received_ref.at[peers], received.at[turn], received_sem.at[turn]),
            pltpu.make_async_copy(left_ref.at[group], left.at[turn], left_sem.at[turn]),
        )

    for turn in range(GROUPS):
        for copy in copies(turn):
            copy.start()
    direct_copy = pltpu.make_async_copy(direct_ref.at[0], direct, direct_sem)
    direct_copy.start()

    def product(turn, values):
        return dot(left[turn], jnp.concatenate(split(values), axis=1))

    for copy in copies(0):
        copy.wait()
    values = received[0].reshape(TERMS, LANES)
    term = lax.broadcasted_iota(jnp.int32, (TERMS, LANES), 0)
    first = (rank - own_group * PEERS) * BLOCK
    below_ref[...] = product(0, jnp.where(term < first, values, 0.0))
    above_ref[...] = product(0, jnp.where(term >= first + BLOCK, values, 0.0))

    def step(turn, _):
        for copy in copies(turn):
            copy.wait()
        values = received[turn].reshape(TERMS, LANES)
        below = own_group + turn >= GROUPS

        @pl.when(below)
        def _():
            below_ref[...] += product(turn, values)

        @pl.when(jnp.logical_not(below))
        def _():
            above_ref[...] += product(turn, values)

        return 0

    lax.fori_loop(1, GROUPS, step, 0)
    direct_copy.wait()
    total = direct[...] - (fold(above_ref[...]) + fold(below_ref[...]).T)
    first_core = lax.rem(rank // COL_DEVICES, CORES) == 0
    for half in range(HALVES):
        start = half * CORES * OUT_ROWS
        zero = total[start : start + OUT_ROWS, :]
        one = total[start + OUT_ROWS : start + 2 * OUT_ROWS, :]
        mine_ref[half] = jnp.where(first_core, zero, one)
        other_ref[half] = jnp.where(first_core, one, zero)


def mirror(rank, left, received, direct):
    return pl.pallas_call(
        mirror_kernel,
        in_specs=[
            pl.BlockSpec(memory_space=pltpu.SMEM),
            pl.BlockSpec(memory_space=pl.ANY),
            pl.BlockSpec(memory_space=pl.ANY),
            pl.BlockSpec(memory_space=pl.ANY),
        ],
        out_specs=[pl.BlockSpec(memory_space=pltpu.VMEM)] * 2,
        out_shape=[jax.ShapeDtypeStruct((HALVES, OUT_ROWS, LANES), jnp.float32)] * 2,
        scratch_shapes=[
            pltpu.VMEM((GROUPS, 2 * LANES, TERMS), jnp.bfloat16),
            pltpu.VMEM((GROUPS, PEERS, BLOCK, LANES), jnp.float32),
            pltpu.VMEM((LANES, LANES), jnp.float32),
            pltpu.VMEM((2 * LANES, 2 * LANES), jnp.float32),
            pltpu.VMEM((2 * LANES, 2 * LANES), jnp.float32),
            pltpu.SemaphoreType.DMA((GROUPS,)),
            pltpu.SemaphoreType.DMA((GROUPS,)),
            pltpu.SemaphoreType.DMA,
        ],
        compiler_params=pltpu.CompilerParams(vmem_limit_bytes=MIRROR_VMEM_LIMIT),
        cost_estimate=pl.CostEstimate(flops=2_500_000_000, bytes_accessed=10_000_000, transcendentals=0),
        name="mirror",
    )(rank, left, received, direct)


def body(cycle_inter, integrals):
    x = jnp.swapaxes(cycle_inter, 0, 1)
    v = jnp.swapaxes(integrals, 0, 1)
    rank = lax.axis_index(AXES).astype(jnp.int32).reshape(1)
    received = lax.all_to_all(pack(rank, x, v), AXES, 0, 0, tiled=True)
    left, direct = local(rank, x, v)
    mine, other = mirror(rank, left, received, direct)
    rows = mine + lax.ppermute(other, "core", [(0, 1), (1, 0)])
    parts = jnp.broadcast_to(rows[:, None], (HALVES, COL_DEVICES, OUT_ROWS, LANES))
    parts = parts.reshape(HALVES * COL_DEVICES, OUT_ROWS, LANES)
    return jnp.sum(lax.all_to_all(parts, CHIPS, 0, 0, tiled=True), axis=0)


def solution(mesh):
    cores = Mesh(mesh.devices.reshape(HALVES, CORES, COL_DEVICES), AXES)
    return jax.shard_map(
        body,
        mesh=cores,
        in_specs=(P(None, AXES, None), P(None, AXES, None)),
        out_specs=P(("half", "core"), None),
        check_vma=False,
    )
```

```python
import jax
import jax.numpy as jnp
from jax import lax
from jax.experimental import pallas as pl
from jax.experimental.pallas import tpu as pltpu
from jax.sharding import Mesh
from jax.sharding import PartitionSpec as P

AXES = ("half", "core", "col")
CHIPS = ("half", "col")
DEVICES = 128
WIDTH = 12
HALF = WIDTH // 2
BLOCK = WIDTH * HALF
LANES = 128
PACK_PEERS = 16
PACK_GROUPS = DEVICES // PACK_PEERS
PACK_PAIRS = PACK_PEERS // 2
PAIR_ROWS = 2 * WIDTH
TILE = 8
PEERS = 32
GROUPS = DEVICES // PEERS
PIECES = ((0, 1536), (1536, 768))
LEFT_GROUPS = 20
DIRECT_LENGTH = 320
ROWS = PEERS * WIDTH
TERMS = PEERS * BLOCK
CORES = 2
HALVES = 8
COL_DEVICES = 8
OUT_ROWS = LANES // (HALVES * CORES)
VMEM_LIMIT = 56 * 1024 * 1024
MIRROR_VMEM_LIMIT = 44 * 1024 * 1024


def split(value):
    high = value.astype(jnp.bfloat16)
    low = (value - high.astype(jnp.float32)).astype(jnp.bfloat16)
    return high, low


def dot(a, b):
    return lax.dot_general(a, b, (((1,), (0,)), ((), ())), preferred_element_type=jnp.float32)


def fold(acc):
    top = acc[:LANES, :LANES] + acc[:LANES, LANES:]
    return top + (acc[LANES:, :LANES] + acc[LANES:, LANES:])


def pack_kernel(rank_ref, x_ref, v_ref, out_ref, rows_ref, own_ref, packed, in_sem, own_sem, out_sem):
    rank = rank_ref[0]
    own_group = rank // PACK_PEERS
    own_half = HALF * (1 - lax.rem(rank, 2))

    def v_copies(group, target, sem):
        source = v_ref.at[pl.ds(own_half, HALF), pl.ds(group * PACK_PAIRS, PACK_PAIRS)]
        return (pltpu.make_async_copy(source, target, sem),)

    def x_copies(group):
        pairs = pl.ds(group * PACK_PAIRS, PACK_PAIRS)
        return tuple(
            pltpu.make_async_copy(
                x_ref.at[:, pairs, pl.ds(start, TILE)], rows_ref.at[group, :, :, pl.ds(start, TILE)], in_sem.at[group, n]
            )
            for n, start in enumerate((0, PAIR_ROWS - TILE))
        )

    def below_copies(group):
        return v_copies(group, rows_ref.at[group, pl.ds(0, HALF)], in_sem.at[group, 0])

    def own_copies():
        return x_copies(own_group) + v_copies(own_group, own_ref, own_sem)

    def pack_v(group, i, source):
        for n in range(HALF):
            rows = source[n, i // 2, pl.ds(WIDTH * (i % 2), WIDTH), :]
            packed[group * PACK_PEERS + i, pl.ds(WIDTH * n, WIDTH), :] = rows

    def pack_x(group, i):
        for c in range(WIDTH):
            rows = rows_ref[group, c, i // 2, pl.ds((WIDTH + HALF) * (i % 2), HALF), :]
            packed[group * PACK_PEERS + i, pl.ds(HALF * c, HALF), :] = rows

    for copy in own_copies():
        copy.start()
    for group in range(PACK_GROUPS):

        @pl.when(group > own_group)
        def _():
            for copy in x_copies(group):
                copy.start()

        @pl.when(group < own_group)
        def _():
            for copy in below_copies(group):
                copy.start()

    def write(group):
        peers = pl.ds(group * PACK_PEERS, PACK_PEERS)
        pltpu.make_async_copy(packed.at[peers], out_ref.at[peers], out_sem).start()

    for copy in own_copies():
        copy.wait()
    for i in range(PACK_PEERS):
        below = own_group * PACK_PEERS + i < rank

        @pl.when(below)
        def _():
            pack_v(own_group, i, own_ref)

        @pl.when(jnp.logical_not(below))
        def _():
            pack_x(own_group, i)

    write(own_group)

    def step(group, _):
        @pl.when(group > own_group)
        def _():
            for copy in x_copies(group):
                copy.wait()
            for i in range(PACK_PEERS):
                pack_x(group, i)
            write(group)

        @pl.when(group < own_group)
        def _():
            for copy in below_copies(group):
                copy.wait()
            for i in range(PACK_PEERS):
                pack_v(group, i, rows_ref.at[group])
            write(group)

        return 0

    lax.fori_loop(0, PACK_GROUPS, step, 0)
    pltpu.make_async_copy(packed, out_ref, out_sem).wait()


def pack(rank, x, v):
    x, v = (array.reshape(WIDTH, DEVICES // 2, PAIR_ROWS, LANES) for array in (x, v))
    return pl.pallas_call(
        pack_kernel,
        in_specs=[
            pl.BlockSpec(memory_space=pltpu.SMEM),
            pl.BlockSpec(memory_space=pl.ANY),
            pl.BlockSpec(memory_space=pl.ANY),
        ],
        out_specs=pl.BlockSpec(memory_space=pl.ANY),
        out_shape=jax.ShapeDtypeStruct((DEVICES, BLOCK, LANES), jnp.float32),
        scratch_shapes=[
            pltpu.VMEM((PACK_GROUPS, WIDTH, PACK_PAIRS, PAIR_ROWS, LANES), jnp.float32),
            pltpu.VMEM((HALF, PACK_PAIRS, PAIR_ROWS, LANES), jnp.float32),
            pltpu.VMEM((DEVICES, BLOCK, LANES), jnp.float32),
            pltpu.SemaphoreType.DMA((PACK_GROUPS, 2)),
            pltpu.SemaphoreType.DMA,
            pltpu.SemaphoreType.DMA,
        ],
        compiler_params=pltpu.CompilerParams(vmem_limit_bytes=VMEM_LIMIT),
        cost_estimate=pl.CostEstimate(flops=0, bytes_accessed=12_000_000, transcendentals=0),
        name="pack",
    )(rank, x, v)


def local_kernel(rank_ref, x_ref, v_ref, left_ref, direct_ref, terms_ref, own_x_ref, own_v_ref, acc_ref):
    rank = rank_ref[0]
    group = pl.program_id(0)
    own_group = rank // PEERS

    @pl.when(group == 0)
    def _():
        acc_ref[...] = jnp.zeros_like(acc_ref)

    own_half = HALF * lax.rem(rank, 2)
    for i in range(PEERS):
        peer = group * PEERS + i

        @pl.when(peer > rank)
        def _():
            start = WIDTH * i + HALF * (1 - i % 2)
            for m in range(WIDTH):
                terms_ref[pl.ds(BLOCK * i + m, HALF, stride=WIDTH), :] = x_ref[m, pl.ds(start, HALF), :]

        @pl.when(peer < rank)
        def _():
            for m in range(HALF):
                rows = v_ref[own_half + m, pl.ds(WIDTH * i, WIDTH), :]
                terms_ref[pl.ds(BLOCK * i + m, WIDTH, stride=HALF), :] = rows

        @pl.when(peer == rank)
        def _():
            terms_ref[pl.ds(BLOCK * i, BLOCK), :] = jnp.zeros((BLOCK, LANES), jnp.float32)
            for c in range(WIDTH):
                own_x_ref[pl.ds(WIDTH * c, WIDTH), :] = x_ref[c, pl.ds(WIDTH * i, WIDTH), :]
                own_v_ref[pl.ds(c, WIDTH, stride=WIDTH), :] = v_ref[c, pl.ds(WIDTH * i, WIDTH), :]

    high, low = split(terms_ref[...].T)
    left_ref[0, :LANES, :] = high
    left_ref[0, LANES:, :] = low

    def add(x_rows, v_rows):
        left = jnp.concatenate(split(x_rows.T), axis=0)
        right = jnp.concatenate(split(v_rows), axis=1)
        acc_ref[...] += dot(left, right)

    @pl.when(group < own_group)
    def _():
        for d in range(WIDTH):
            add(x_ref[d], v_ref[d])

    @pl.when(group == own_group)
    def _():
        ids = group * ROWS + lax.broadcasted_iota(jnp.int32, (ROWS, LANES), 0)
        for d in range(WIDTH):
            add(x_ref[d], jnp.where(ids < rank * WIDTH + d, v_ref[d], 0.0))
        pair = lax.broadcasted_iota(jnp.int32, (WIDTH * WIDTH, LANES), 0)
        upper = pair % WIDTH > pair // WIDTH
        add(own_x_ref[...], jnp.where(upper, -own_v_ref[...], 0.0))

    @pl.when(group == GROUPS - 1)
    def _():
        direct_ref[0] = fold(acc_ref[...])


def local(rank, x, v):
    return pl.pallas_call(
        local_kernel,
        grid_spec=pltpu.PrefetchScalarGridSpec(
            num_scalar_prefetch=1,
            grid=(GROUPS,),
            in_specs=[
                pl.BlockSpec((WIDTH, ROWS, LANES), lambda g, r: (0, g, 0)),
                pl.BlockSpec((WIDTH, ROWS, LANES), lambda g, r: (0, jnp.minimum(g, r[0] // PEERS), 0)),
            ],
            out_specs=[
                pl.BlockSpec((1, 2 * LANES, TERMS), lambda g, r: (g, 0, 0)),
                pl.BlockSpec((1, LANES, LANES), lambda g, r: (0, 0, 0)),
            ],
            scratch_shapes=[
                pltpu.VMEM((TERMS, LANES), jnp.float32),
                pltpu.VMEM((WIDTH * WIDTH, LANES), jnp.float32),
                pltpu.VMEM((WIDTH * WIDTH, LANES), jnp.float32),
                pltpu.VMEM((2 * LANES, 2 * LANES), jnp.float32),
            ],
        ),
        out_shape=[
            jax.ShapeDtypeStruct((LEFT_GROUPS, 2 * LANES, TERMS), jnp.bfloat16),
            jax.ShapeDtypeStruct((DIRECT_LENGTH, LANES, LANES), jnp.float32),
        ],
        compiler_params=pltpu.CompilerParams(vmem_limit_bytes=VMEM_LIMIT),
        cost_estimate=pl.CostEstimate(flops=20_000_000_000, bytes_accessed=30_000_000, transcendentals=0),
        name="local",
    )(rank, x, v)


def mirror_kernel(
    rank_ref,
    left_ref,
    received_ref,
    direct_ref,
    mine_ref,
    other_ref,
    left,
    received,
    direct,
    below_ref,
    above_ref,
    left_sem,
    received_sem,
    direct_sem,
):
    rank = rank_ref[0]
    own_group = rank // PEERS

    last = GROUPS - 1

    def copies(turn, start=0, length=TERMS, sem=None):
        group = lax.rem(own_group + turn, GROUPS)
        sem = turn if sem is None else sem
        terms = pl.ds(start, length)
        rows = received_ref.at[pl.ds(group * TERMS + start, length)]
        return (
            pltpu.make_async_copy(rows, received.at[turn, terms], received_sem.at[sem]),
            pltpu.make_async_copy(left_ref.at[group, :, terms], left.at[turn, :, terms], left_sem.at[sem]),
        )

    def last_copies(piece):
        return copies(last, *PIECES[piece], last + piece)

    for turn in range(last):
        for copy in copies(turn):
            copy.start()
    for piece in range(len(PIECES)):
        for copy in last_copies(piece):
            copy.start()
    direct_copy = pltpu.make_async_copy(direct_ref.at[0], direct, direct_sem)
    direct_copy.start()

    def product(turn, values):
        return dot(left[turn], jnp.concatenate(split(values), axis=1))

    for copy in copies(0):
        copy.wait()
    values = received[0]
    term = lax.broadcasted_iota(jnp.int32, (TERMS, LANES), 0)
    first = (rank - own_group * PEERS) * BLOCK
    below_ref[...] = product(0, jnp.where(term < first, values, 0.0))
    above_ref[...] = product(0, jnp.where(term >= first + BLOCK, values, 0.0))

    def step(turn, _):
        for copy in copies(turn):
            copy.wait()
        values = received[turn]
        below = own_group + turn >= GROUPS

        @pl.when(below)
        def _():
            below_ref[...] += product(turn, values)

        @pl.when(jnp.logical_not(below))
        def _():
            above_ref[...] += product(turn, values)

        return 0

    lax.fori_loop(1, last, step, 0)
    for piece, (start, length) in enumerate(PIECES):
        for copy in last_copies(piece):
            copy.wait()
        terms = pl.ds(start, length)
        right = jnp.concatenate(split(received[last, terms]), axis=1)
        part = dot(left[last, :, terms], right)
        below = own_group + last >= GROUPS

        @pl.when(below)
        def _():
            below_ref[...] += part

        @pl.when(jnp.logical_not(below))
        def _():
            above_ref[...] += part

    direct_copy.wait()
    total = direct[...] - (fold(above_ref[...]) + fold(below_ref[...]).T)
    first_core = lax.rem(rank // COL_DEVICES, CORES) == 0
    for half in range(HALVES):
        start = half * CORES * OUT_ROWS
        zero = total[start : start + OUT_ROWS, :]
        one = total[start + OUT_ROWS : start + 2 * OUT_ROWS, :]
        mine_ref[half] = jnp.where(first_core, zero, one)
        other_ref[half] = jnp.where(first_core, one, zero)


def mirror(rank, left, received, direct):
    return pl.pallas_call(
        mirror_kernel,
        in_specs=[
            pl.BlockSpec(memory_space=pltpu.SMEM),
            pl.BlockSpec(memory_space=pl.ANY),
            pl.BlockSpec(memory_space=pl.ANY),
            pl.BlockSpec(memory_space=pl.ANY),
        ],
        out_specs=[pl.BlockSpec(memory_space=pltpu.VMEM)] * 2,
        out_shape=[jax.ShapeDtypeStruct((HALVES, OUT_ROWS, LANES), jnp.float32)] * 2,
        scratch_shapes=[
            pltpu.VMEM((GROUPS, 2 * LANES, TERMS), jnp.bfloat16),
            pltpu.VMEM((GROUPS, TERMS, LANES), jnp.float32),
            pltpu.VMEM((LANES, LANES), jnp.float32),
            pltpu.VMEM((2 * LANES, 2 * LANES), jnp.float32),
            pltpu.VMEM((2 * LANES, 2 * LANES), jnp.float32),
            pltpu.SemaphoreType.DMA((GROUPS - 1 + len(PIECES),)),
            pltpu.SemaphoreType.DMA((GROUPS - 1 + len(PIECES),)),
            pltpu.SemaphoreType.DMA,
        ],
        compiler_params=pltpu.CompilerParams(vmem_limit_bytes=MIRROR_VMEM_LIMIT),
        cost_estimate=pl.CostEstimate(flops=2_500_000_000, bytes_accessed=10_000_000, transcendentals=0),
        name="mirror",
    )(rank, left, received.reshape(DEVICES * BLOCK, LANES), direct)


def body(cycle_inter, integrals):
    x = jnp.swapaxes(cycle_inter, 0, 1)
    v = jnp.swapaxes(integrals, 0, 1)
    rank = lax.axis_index(AXES).astype(jnp.int32).reshape(1)
    received = lax.all_to_all(pack(rank, x, v), AXES, 0, 0, tiled=True)
    left, direct = local(rank, x, v)
    mine, other = mirror(rank, left, received, direct)
    rows = mine + lax.ppermute(other, "core", [(0, 1), (1, 0)])
    parts = jnp.broadcast_to(rows[:, None], (HALVES, COL_DEVICES, OUT_ROWS, LANES))
    parts = parts.reshape(HALVES * COL_DEVICES, OUT_ROWS, LANES)
    return jnp.sum(lax.all_to_all(parts, CHIPS, 0, 0, tiled=True), axis=0)


def solution(mesh):
    cores = Mesh(mesh.devices.reshape(HALVES, CORES, COL_DEVICES), AXES)
    return jax.shard_map(
        body,
        mesh=cores,
        in_specs=(P(None, AXES, None), P(None, AXES, None)),
        out_specs=P(("half", "core"), None),
        check_vma=False,
    )
```

```python
import jax
import jax.numpy as jnp
from jax import lax
from jax.experimental import pallas as pl
from jax.experimental.pallas import tpu as pltpu
from jax.sharding import Mesh
from jax.sharding import PartitionSpec as P

AXES = ("half", "core", "col")
CHIPS = ("half", "col")
DEVICES = 128
WIDTH = 12
HALF = WIDTH // 2
BLOCK = WIDTH * HALF
LANES = 128
PACK_PEERS = 16
PACK_GROUPS = DEVICES // PACK_PEERS
PACK_PAIRS = PACK_PEERS // 2
PAIR_ROWS = 2 * WIDTH
TILE = 8
PEERS = 32
GROUPS = DEVICES // PEERS
LEFT_GROUPS = 20
DIRECT_LENGTH = 320
ROWS = PEERS * WIDTH
TERMS = PEERS * BLOCK
CORES = 2
HALVES = 8
COL_DEVICES = 8
OUT_ROWS = LANES // (HALVES * CORES)
VMEM_LIMIT = 56 * 1024 * 1024
MIRROR_VMEM_LIMIT = 44 * 1024 * 1024


def split(value):
    high = value.astype(jnp.bfloat16)
    low = (value - high.astype(jnp.float32)).astype(jnp.bfloat16)
    return high, low


def dot(a, b):
    return lax.dot_general(a, b, (((1,), (0,)), ((), ())), preferred_element_type=jnp.float32)


def fold(acc):
    top = acc[:LANES, :LANES] + acc[:LANES, LANES:]
    return top + (acc[LANES:, :LANES] + acc[LANES:, LANES:])


def pack_kernel(rank_ref, x_ref, v_ref, out_ref, rows_ref, own_ref, packed, in_sem, own_sem, out_sem):
    rank = rank_ref[0]
    own_group = rank // PACK_PEERS
    own_half = HALF * (1 - lax.rem(rank, 2))

    def v_copies(group, target, sem):
        source = v_ref.at[pl.ds(own_half, HALF), pl.ds(group * PACK_PAIRS, PACK_PAIRS)]
        return (pltpu.make_async_copy(source, target, sem),)

    def x_copies(group):
        pairs = pl.ds(group * PACK_PAIRS, PACK_PAIRS)
        return tuple(
            pltpu.make_async_copy(
                x_ref.at[:, pairs, pl.ds(start, TILE)], rows_ref.at[group, :, :, pl.ds(start, TILE)], in_sem.at[group, n]
            )
            for n, start in enumerate((0, PAIR_ROWS - TILE))
        )

    def below_copies(group):
        return v_copies(group, rows_ref.at[group, pl.ds(0, HALF)], in_sem.at[group, 0])

    def own_copies():
        return x_copies(own_group) + v_copies(own_group, own_ref, own_sem)

    def pack_v(group, pair, odd, source):
        for n in range(HALF):
            rows = source[n, pair, pl.ds(WIDTH * odd, WIDTH), :]
            packed[group * PACK_PEERS + 2 * pair + odd, pl.ds(WIDTH * n, WIDTH), :] = rows

    def pack_x(group, pair, odd):
        for c in range(WIDTH):
            rows = rows_ref[group, c, pair, pl.ds((WIDTH + HALF) * odd, HALF), :]
            packed[group * PACK_PEERS + 2 * pair + odd, pl.ds(HALF * c, HALF), :] = rows

    def over_peers(move):
        def pair_step(pair, _):
            for odd in range(2):
                move(pair, odd)
            return 0

        lax.fori_loop(0, PACK_PAIRS, pair_step, 0)

    for copy in own_copies():
        copy.start()
    for group in range(PACK_GROUPS):

        @pl.when(group > own_group)
        def _():
            for copy in x_copies(group):
                copy.start()

        @pl.when(group < own_group)
        def _():
            for copy in below_copies(group):
                copy.start()

    def write(group):
        peers = pl.ds(group * PACK_PEERS, PACK_PEERS)
        pltpu.make_async_copy(packed.at[peers], out_ref.at[peers], out_sem).start()

    for copy in own_copies():
        copy.wait()

    def pack_own(pair, odd):
        below = own_group * PACK_PEERS + 2 * pair + odd < rank

        @pl.when(below)
        def _():
            pack_v(own_group, pair, odd, own_ref)

        @pl.when(jnp.logical_not(below))
        def _():
            pack_x(own_group, pair, odd)

    over_peers(pack_own)
    write(own_group)

    def step(group, _):
        @pl.when(group > own_group)
        def _():
            for copy in x_copies(group):
                copy.wait()
            over_peers(lambda pair, odd: pack_x(group, pair, odd))
            write(group)

        @pl.when(group < own_group)
        def _():
            for copy in below_copies(group):
                copy.wait()
            over_peers(lambda pair, odd: pack_v(group, pair, odd, rows_ref.at[group]))
            write(group)

        return 0

    lax.fori_loop(0, PACK_GROUPS, step, 0)
    pltpu.make_async_copy(packed, out_ref, out_sem).wait()


def pack(rank, x, v):
    x, v = (array.reshape(WIDTH, DEVICES // 2, PAIR_ROWS, LANES) for array in (x, v))
    return pl.pallas_call(
        pack_kernel,
        in_specs=[
            pl.BlockSpec(memory_space=pltpu.SMEM),
            pl.BlockSpec(memory_space=pl.ANY),
            pl.BlockSpec(memory_space=pl.ANY),
        ],
        out_specs=pl.BlockSpec(memory_space=pl.ANY),
        out_shape=jax.ShapeDtypeStruct((DEVICES, BLOCK, LANES), jnp.float32),
        scratch_shapes=[
            pltpu.VMEM((PACK_GROUPS, WIDTH, PACK_PAIRS, PAIR_ROWS, LANES), jnp.float32),
            pltpu.VMEM((HALF, PACK_PAIRS, PAIR_ROWS, LANES), jnp.float32),
            pltpu.VMEM((DEVICES, BLOCK, LANES), jnp.float32),
            pltpu.SemaphoreType.DMA((PACK_GROUPS, 2)),
            pltpu.SemaphoreType.DMA,
            pltpu.SemaphoreType.DMA,
        ],
        compiler_params=pltpu.CompilerParams(vmem_limit_bytes=VMEM_LIMIT),
        cost_estimate=pl.CostEstimate(flops=0, bytes_accessed=12_000_000, transcendentals=0),
        name="pack",
    )(rank, x, v)


def local_kernel(rank_ref, x_ref, v_ref, left_ref, direct_ref, terms_ref, own_x_ref, own_v_ref, acc_ref):
    rank = rank_ref[0]
    group = pl.program_id(0)
    own_group = rank // PEERS

    @pl.when(group == 0)
    def _():
        acc_ref[...] = jnp.zeros_like(acc_ref)

    own_half = HALF * lax.rem(rank, 2)
    for i in range(PEERS):
        peer = group * PEERS + i

        @pl.when(peer > rank)
        def _():
            start = WIDTH * i + HALF * (1 - i % 2)
            for m in range(WIDTH):
                terms_ref[pl.ds(BLOCK * i + m, HALF, stride=WIDTH), :] = x_ref[m, pl.ds(start, HALF), :]

        @pl.when(peer < rank)
        def _():
            for m in range(HALF):
                rows = v_ref[own_half + m, pl.ds(WIDTH * i, WIDTH), :]
                terms_ref[pl.ds(BLOCK * i + m, WIDTH, stride=HALF), :] = rows

        @pl.when(peer == rank)
        def _():
            terms_ref[pl.ds(BLOCK * i, BLOCK), :] = jnp.zeros((BLOCK, LANES), jnp.float32)
            for c in range(WIDTH):
                own_x_ref[pl.ds(WIDTH * c, WIDTH), :] = x_ref[c, pl.ds(WIDTH * i, WIDTH), :]
                own_v_ref[pl.ds(c, WIDTH, stride=WIDTH), :] = v_ref[c, pl.ds(WIDTH * i, WIDTH), :]

    high, low = split(terms_ref[...].T)
    left_ref[0, :LANES, :] = high
    left_ref[0, LANES:, :] = low

    def add(x_rows, v_rows):
        left = jnp.concatenate(split(x_rows.T), axis=0)
        right = jnp.concatenate(split(v_rows), axis=1)
        acc_ref[...] += dot(left, right)

    @pl.when(group < own_group)
    def _():
        for d in range(WIDTH):
            add(x_ref[d], v_ref[d])

    @pl.when(group == own_group)
    def _():
        ids = group * ROWS + lax.broadcasted_iota(jnp.int32, (ROWS, LANES), 0)
        for d in range(WIDTH):
            add(x_ref[d], jnp.where(ids < rank * WIDTH + d, v_ref[d], 0.0))
        pair = lax.broadcasted_iota(jnp.int32, (WIDTH * WIDTH, LANES), 0)
        upper = pair % WIDTH > pair // WIDTH
        add(own_x_ref[...], jnp.where(upper, -own_v_ref[...], 0.0))

    @pl.when(group == GROUPS - 1)
    def _():
        direct_ref[0] = fold(acc_ref[...])


def local(rank, x, v):
    return pl.pallas_call(
        local_kernel,
        grid_spec=pltpu.PrefetchScalarGridSpec(
            num_scalar_prefetch=1,
            grid=(GROUPS,),
            in_specs=[
                pl.BlockSpec((WIDTH, ROWS, LANES), lambda g, r: (0, g, 0)),
                pl.BlockSpec((WIDTH, ROWS, LANES), lambda g, r: (0, jnp.minimum(g, r[0] // PEERS), 0)),
            ],
            out_specs=[
                pl.BlockSpec((1, 2 * LANES, TERMS), lambda g, r: (g, 0, 0)),
                pl.BlockSpec((1, LANES, LANES), lambda g, r: (0, 0, 0)),
            ],
            scratch_shapes=[
                pltpu.VMEM((TERMS, LANES), jnp.float32),
                pltpu.VMEM((WIDTH * WIDTH, LANES), jnp.float32),
                pltpu.VMEM((WIDTH * WIDTH, LANES), jnp.float32),
                pltpu.VMEM((2 * LANES, 2 * LANES), jnp.float32),
            ],
        ),
        out_shape=[
            jax.ShapeDtypeStruct((LEFT_GROUPS, 2 * LANES, TERMS), jnp.bfloat16),
            jax.ShapeDtypeStruct((DIRECT_LENGTH, LANES, LANES), jnp.float32),
        ],
        compiler_params=pltpu.CompilerParams(vmem_limit_bytes=VMEM_LIMIT),
        cost_estimate=pl.CostEstimate(flops=20_000_000_000, bytes_accessed=30_000_000, transcendentals=0),
        name="local",
    )(rank, x, v)


def mirror_kernel(
    rank_ref,
    left_ref,
    received_ref,
    direct_ref,
    mine_ref,
    other_ref,
    left,
    received,
    direct,
    below_ref,
    above_ref,
    left_sem,
    received_sem,
    direct_sem,
):
    rank = rank_ref[0]
    own_group = rank // PEERS

    def copies(turn):
        group = lax.rem(own_group + turn, GROUPS)
        peers = pl.ds(group * PEERS, PEERS)
        return (
            pltpu.make_async_copy(received_ref.at[peers], received.at[turn], received_sem.at[turn]),
            pltpu.make_async_copy(left_ref.at[group], left.at[turn], left_sem.at[turn]),
        )

    for turn in range(GROUPS):
        for copy in copies(turn):
            copy.start()
    direct_copy = pltpu.make_async_copy(direct_ref.at[0], direct, direct_sem)
    direct_copy.start()

    def product(turn, values):
        return dot(left[turn], jnp.concatenate(split(values), axis=1))

    for copy in copies(0):
        copy.wait()
    values = received[0].reshape(TERMS, LANES)
    term = lax.broadcasted_iota(jnp.int32, (TERMS, LANES), 0)
    first = (rank - own_group * PEERS) * BLOCK
    below_ref[...] = product(0, jnp.where(term < first, values, 0.0))
    above_ref[...] = product(0, jnp.where(term >= first + BLOCK, values, 0.0))

    def step(turn, _):
        for copy in copies(turn):
            copy.wait()
        values = received[turn].reshape(TERMS, LANES)
        below = own_group + turn >= GROUPS

        @pl.when(below)
        def _():
            below_ref[...] += product(turn, values)

        @pl.when(jnp.logical_not(below))
        def _():
            above_ref[...] += product(turn, values)

        return 0

    lax.fori_loop(1, GROUPS, step, 0)
    direct_copy.wait()
    total = direct[...] - (fold(above_ref[...]) + fold(below_ref[...]).T)
    first_core = lax.rem(rank // COL_DEVICES, CORES) == 0
    for half in range(HALVES):
        start = half * CORES * OUT_ROWS
        zero = total[start : start + OUT_ROWS, :]
        one = total[start + OUT_ROWS : start + 2 * OUT_ROWS, :]
        mine_ref[half] = jnp.where(first_core, zero, one)
        other_ref[half] = jnp.where(first_core, one, zero)


def mirror(rank, left, received, direct):
    return pl.pallas_call(
        mirror_kernel,
        in_specs=[
            pl.BlockSpec(memory_space=pltpu.SMEM),
            pl.BlockSpec(memory_space=pl.ANY),
            pl.BlockSpec(memory_space=pl.ANY),
            pl.BlockSpec(memory_space=pl.ANY),
        ],
        out_specs=[pl.BlockSpec(memory_space=pltpu.VMEM)] * 2,
        out_shape=[jax.ShapeDtypeStruct((HALVES, OUT_ROWS, LANES), jnp.float32)] * 2,
        scratch_shapes=[
            pltpu.VMEM((GROUPS, 2 * LANES, TERMS), jnp.bfloat16),
            pltpu.VMEM((GROUPS, PEERS, BLOCK, LANES), jnp.float32),
            pltpu.VMEM((LANES, LANES), jnp.float32),
            pltpu.VMEM((2 * LANES, 2 * LANES), jnp.float32),
            pltpu.VMEM((2 * LANES, 2 * LANES), jnp.float32),
            pltpu.SemaphoreType.DMA((GROUPS,)),
            pltpu.SemaphoreType.DMA((GROUPS,)),
            pltpu.SemaphoreType.DMA,
        ],
        compiler_params=pltpu.CompilerParams(vmem_limit_bytes=MIRROR_VMEM_LIMIT),
        cost_estimate=pl.CostEstimate(flops=2_500_000_000, bytes_accessed=10_000_000, transcendentals=0),
        name="mirror",
    )(rank, left, received, direct)


def body(cycle_inter, integrals):
    x = jnp.swapaxes(cycle_inter, 0, 1)
    v = jnp.swapaxes(integrals, 0, 1)
    rank = lax.axis_index(AXES).astype(jnp.int32).reshape(1)
    received = lax.all_to_all(pack(rank, x, v), AXES, 0, 0, tiled=True)
    left, direct = local(rank, x, v)
    mine, other = mirror(rank, left, received, direct)
    rows = mine + lax.ppermute(other, "core", [(0, 1), (1, 0)])
    parts = jnp.broadcast_to(rows[:, None], (HALVES, COL_DEVICES, OUT_ROWS, LANES))
    parts = parts.reshape(HALVES * COL_DEVICES, OUT_ROWS, LANES)
    return jnp.sum(lax.all_to_all(parts, CHIPS, 0, 0, tiled=True), axis=0)


def solution(mesh):
    cores = Mesh(mesh.devices.reshape(HALVES, CORES, COL_DEVICES), AXES)
    return jax.shard_map(
        body,
        mesh=cores,
        in_specs=(P(None, AXES, None), P(None, AXES, None)),
        out_specs=P(("half", "core"), None),
        check_vma=False,
    )
```

```python
import jax
import jax.numpy as jnp
from jax import lax
from jax.experimental import pallas as pl
from jax.experimental.pallas import tpu as pltpu
from jax.sharding import Mesh
from jax.sharding import PartitionSpec as P

AXES = ("half", "core", "col")
CHIPS = ("half", "col")
DEVICES = 128
WIDTH = 12
HALF = WIDTH // 2
BLOCK = WIDTH * HALF
LANES = 128
PACK_PEERS = 32
PACK_GROUPS = DEVICES // PACK_PEERS
PACK_PAIRS = PACK_PEERS // 2
PAIR_ROWS = 2 * WIDTH
TILE = 8
PEERS = 32
GROUPS = DEVICES // PEERS
LEFT_GROUPS = 20
DIRECT_LENGTH = 320
ROWS = PEERS * WIDTH
TERMS = PEERS * BLOCK
CORES = 2
HALVES = 8
COL_DEVICES = 8
OUT_ROWS = LANES // (HALVES * CORES)
VMEM_LIMIT = 56 * 1024 * 1024
MIRROR_VMEM_LIMIT = 44 * 1024 * 1024


def split(value):
    high = value.astype(jnp.bfloat16)
    low = (value - high.astype(jnp.float32)).astype(jnp.bfloat16)
    return high, low


def dot(a, b):
    return lax.dot_general(a, b, (((1,), (0,)), ((), ())), preferred_element_type=jnp.float32)


def fold(acc):
    top = acc[:LANES, :LANES] + acc[:LANES, LANES:]
    return top + (acc[LANES:, :LANES] + acc[LANES:, LANES:])


def pack_kernel(rank_ref, x_ref, v_ref, out_ref, rows_ref, own_ref, packed, in_sem, own_sem, out_sem):
    rank = rank_ref[0]
    own_group = rank // PACK_PEERS
    own_half = HALF * (1 - lax.rem(rank, 2))

    def v_copies(group, target, sem):
        source = v_ref.at[pl.ds(own_half, HALF), pl.ds(group * PACK_PAIRS, PACK_PAIRS)]
        return (pltpu.make_async_copy(source, target, sem),)

    def x_copies(group):
        pairs = pl.ds(group * PACK_PAIRS, PACK_PAIRS)
        return tuple(
            pltpu.make_async_copy(
                x_ref.at[:, pairs, pl.ds(start, TILE)], rows_ref.at[group, :, :, pl.ds(start, TILE)], in_sem.at[group, n]
            )
            for n, start in enumerate((0, PAIR_ROWS - TILE))
        )

    def below_copies(group):
        return v_copies(group, rows_ref.at[group, pl.ds(0, HALF)], in_sem.at[group, 0])

    def own_copies():
        return x_copies(own_group) + v_copies(own_group, own_ref, own_sem)

    def pack_v(group, pair, odd, source):
        for n in range(HALF):
            rows = source[n, pair, pl.ds(WIDTH * odd, WIDTH), :]
            packed[group * PACK_PEERS + 2 * pair + odd, pl.ds(WIDTH * n, WIDTH), :] = rows

    def pack_x(group, pair, odd):
        for c in range(WIDTH):
            rows = rows_ref[group, c, pair, pl.ds((WIDTH + HALF) * odd, HALF), :]
            packed[group * PACK_PEERS + 2 * pair + odd, pl.ds(HALF * c, HALF), :] = rows

    def over_peers(move):
        def pair_step(pair, _):
            for odd in range(2):
                move(pair, odd)
            return 0

        lax.fori_loop(0, PACK_PAIRS, pair_step, 0)

    for copy in own_copies():
        copy.start()
    for group in range(PACK_GROUPS):

        @pl.when(group > own_group)
        def _():
            for copy in x_copies(group):
                copy.start()

        @pl.when(group < own_group)
        def _():
            for copy in below_copies(group):
                copy.start()

    def write(group):
        peers = pl.ds(group * PACK_PEERS, PACK_PEERS)
        pltpu.make_async_copy(packed.at[peers], out_ref.at[peers], out_sem).start()

    for copy in own_copies():
        copy.wait()

    def pack_own(pair, odd):
        below = own_group * PACK_PEERS + 2 * pair + odd < rank

        @pl.when(below)
        def _():
            pack_v(own_group, pair, odd, own_ref)

        @pl.when(jnp.logical_not(below))
        def _():
            pack_x(own_group, pair, odd)

    over_peers(pack_own)
    write(own_group)

    def step(group, _):
        @pl.when(group > own_group)
        def _():
            for copy in x_copies(group):
                copy.wait()
            over_peers(lambda pair, odd: pack_x(group, pair, odd))
            write(group)

        @pl.when(group < own_group)
        def _():
            for copy in below_copies(group):
                copy.wait()
            over_peers(lambda pair, odd: pack_v(group, pair, odd, rows_ref.at[group]))
            write(group)

        return 0

    lax.fori_loop(0, PACK_GROUPS, step, 0)
    pltpu.make_async_copy(packed, out_ref, out_sem).wait()


def pack(rank, x, v):
    x, v = (array.reshape(WIDTH, DEVICES // 2, PAIR_ROWS, LANES) for array in (x, v))
    return pl.pallas_call(
        pack_kernel,
        in_specs=[
            pl.BlockSpec(memory_space=pltpu.SMEM),
            pl.BlockSpec(memory_space=pl.ANY),
            pl.BlockSpec(memory_space=pl.ANY),
        ],
        out_specs=pl.BlockSpec(memory_space=pl.ANY),
        out_shape=jax.ShapeDtypeStruct((DEVICES, BLOCK, LANES), jnp.float32),
        scratch_shapes=[
            pltpu.VMEM((PACK_GROUPS, WIDTH, PACK_PAIRS, PAIR_ROWS, LANES), jnp.float32),
            pltpu.VMEM((HALF, PACK_PAIRS, PAIR_ROWS, LANES), jnp.float32),
            pltpu.VMEM((DEVICES, BLOCK, LANES), jnp.float32),
            pltpu.SemaphoreType.DMA((PACK_GROUPS, 2)),
            pltpu.SemaphoreType.DMA,
            pltpu.SemaphoreType.DMA,
        ],
        compiler_params=pltpu.CompilerParams(vmem_limit_bytes=VMEM_LIMIT),
        cost_estimate=pl.CostEstimate(flops=0, bytes_accessed=12_000_000, transcendentals=0),
        name="pack",
    )(rank, x, v)


def local_kernel(rank_ref, x_ref, v_ref, left_ref, direct_ref, terms_ref, own_x_ref, own_v_ref, acc_ref):
    rank = rank_ref[0]
    group = pl.program_id(0)
    own_group = rank // PEERS

    @pl.when(group == 0)
    def _():
        acc_ref[...] = jnp.zeros_like(acc_ref)

    own_half = HALF * lax.rem(rank, 2)
    for i in range(PEERS):
        peer = group * PEERS + i

        @pl.when(peer > rank)
        def _():
            start = WIDTH * i + HALF * (1 - i % 2)
            for m in range(WIDTH):
                terms_ref[pl.ds(BLOCK * i + m, HALF, stride=WIDTH), :] = x_ref[m, pl.ds(start, HALF), :]

        @pl.when(peer < rank)
        def _():
            for m in range(HALF):
                rows = v_ref[own_half + m, pl.ds(WIDTH * i, WIDTH), :]
                terms_ref[pl.ds(BLOCK * i + m, WIDTH, stride=HALF), :] = rows

        @pl.when(peer == rank)
        def _():
            terms_ref[pl.ds(BLOCK * i, BLOCK), :] = jnp.zeros((BLOCK, LANES), jnp.float32)
            for c in range(WIDTH):
                own_x_ref[pl.ds(WIDTH * c, WIDTH), :] = x_ref[c, pl.ds(WIDTH * i, WIDTH), :]
                own_v_ref[pl.ds(c, WIDTH, stride=WIDTH), :] = v_ref[c, pl.ds(WIDTH * i, WIDTH), :]

    high, low = split(terms_ref[...].T)
    left_ref[0, :LANES, :] = high
    left_ref[0, LANES:, :] = low

    def add(x_rows, v_rows):
        left = jnp.concatenate(split(x_rows.T), axis=0)
        right = jnp.concatenate(split(v_rows), axis=1)
        acc_ref[...] += dot(left, right)

    @pl.when(group < own_group)
    def _():
        for d in range(WIDTH):
            add(x_ref[d], v_ref[d])

    @pl.when(group == own_group)
    def _():
        ids = group * ROWS + lax.broadcasted_iota(jnp.int32, (ROWS, LANES), 0)
        for d in range(WIDTH):
            add(x_ref[d], jnp.where(ids < rank * WIDTH + d, v_ref[d], 0.0))
        pair = lax.broadcasted_iota(jnp.int32, (WIDTH * WIDTH, LANES), 0)
        upper = pair % WIDTH > pair // WIDTH
        add(own_x_ref[...], jnp.where(upper, -own_v_ref[...], 0.0))

    @pl.when(group == GROUPS - 1)
    def _():
        direct_ref[0] = fold(acc_ref[...])


def local(rank, x, v):
    return pl.pallas_call(
        local_kernel,
        grid_spec=pltpu.PrefetchScalarGridSpec(
            num_scalar_prefetch=1,
            grid=(GROUPS,),
            in_specs=[
                pl.BlockSpec((WIDTH, ROWS, LANES), lambda g, r: (0, g, 0)),
                pl.BlockSpec((WIDTH, ROWS, LANES), lambda g, r: (0, jnp.minimum(g, r[0] // PEERS), 0)),
            ],
            out_specs=[
                pl.BlockSpec((1, 2 * LANES, TERMS), lambda g, r: (g, 0, 0)),
                pl.BlockSpec((1, LANES, LANES), lambda g, r: (0, 0, 0)),
            ],
            scratch_shapes=[
                pltpu.VMEM((TERMS, LANES), jnp.float32),
                pltpu.VMEM((WIDTH * WIDTH, LANES), jnp.float32),
                pltpu.VMEM((WIDTH * WIDTH, LANES), jnp.float32),
                pltpu.VMEM((2 * LANES, 2 * LANES), jnp.float32),
            ],
        ),
        out_shape=[
            jax.ShapeDtypeStruct((LEFT_GROUPS, 2 * LANES, TERMS), jnp.bfloat16),
            jax.ShapeDtypeStruct((DIRECT_LENGTH, LANES, LANES), jnp.float32),
        ],
        compiler_params=pltpu.CompilerParams(vmem_limit_bytes=VMEM_LIMIT),
        cost_estimate=pl.CostEstimate(flops=20_000_000_000, bytes_accessed=30_000_000, transcendentals=0),
        name="local",
    )(rank, x, v)


def mirror_kernel(
    rank_ref,
    left_ref,
    received_ref,
    direct_ref,
    mine_ref,
    other_ref,
    left,
    received,
    direct,
    below_ref,
    above_ref,
    left_sem,
    received_sem,
    direct_sem,
):
    rank = rank_ref[0]
    own_group = rank // PEERS

    def copies(turn):
        group = lax.rem(own_group + turn, GROUPS)
        peers = pl.ds(group * PEERS, PEERS)
        return (
            pltpu.make_async_copy(received_ref.at[peers], received.at[turn], received_sem.at[turn]),
            pltpu.make_async_copy(left_ref.at[group], left.at[turn], left_sem.at[turn]),
        )

    for turn in range(GROUPS):
        for copy in copies(turn):
            copy.start()
    direct_copy = pltpu.make_async_copy(direct_ref.at[0], direct, direct_sem)
    direct_copy.start()

    def product(turn, values):
        return dot(left[turn], jnp.concatenate(split(values), axis=1))

    for copy in copies(0):
        copy.wait()
    values = received[0].reshape(TERMS, LANES)
    term = lax.broadcasted_iota(jnp.int32, (TERMS, LANES), 0)
    first = (rank - own_group * PEERS) * BLOCK
    below_ref[...] = product(0, jnp.where(term < first, values, 0.0))
    above_ref[...] = product(0, jnp.where(term >= first + BLOCK, values, 0.0))

    def step(turn, _):
        for copy in copies(turn):
            copy.wait()
        values = received[turn].reshape(TERMS, LANES)
        below = own_group + turn >= GROUPS

        @pl.when(below)
        def _():
            below_ref[...] += product(turn, values)

        @pl.when(jnp.logical_not(below))
        def _():
            above_ref[...] += product(turn, values)

        return 0

    lax.fori_loop(1, GROUPS, step, 0)
    direct_copy.wait()
    total = direct[...] - (fold(above_ref[...]) + fold(below_ref[...]).T)
    first_core = lax.rem(rank // COL_DEVICES, CORES) == 0
    for half in range(HALVES):
        start = half * CORES * OUT_ROWS
        zero = total[start : start + OUT_ROWS, :]
        one = total[start + OUT_ROWS : start + 2 * OUT_ROWS, :]
        mine_ref[half] = jnp.where(first_core, zero, one)
        other_ref[half] = jnp.where(first_core, one, zero)


def mirror(rank, left, received, direct):
    return pl.pallas_call(
        mirror_kernel,
        in_specs=[
            pl.BlockSpec(memory_space=pltpu.SMEM),
            pl.BlockSpec(memory_space=pl.ANY),
            pl.BlockSpec(memory_space=pl.ANY),
            pl.BlockSpec(memory_space=pl.ANY),
        ],
        out_specs=[pl.BlockSpec(memory_space=pltpu.VMEM)] * 2,
        out_shape=[jax.ShapeDtypeStruct((HALVES, OUT_ROWS, LANES), jnp.float32)] * 2,
        scratch_shapes=[
            pltpu.VMEM((GROUPS, 2 * LANES, TERMS), jnp.bfloat16),
            pltpu.VMEM((GROUPS, PEERS, BLOCK, LANES), jnp.float32),
            pltpu.VMEM((LANES, LANES), jnp.float32),
            pltpu.VMEM((2 * LANES, 2 * LANES), jnp.float32),
            pltpu.VMEM((2 * LANES, 2 * LANES), jnp.float32),
            pltpu.SemaphoreType.DMA((GROUPS,)),
            pltpu.SemaphoreType.DMA((GROUPS,)),
            pltpu.SemaphoreType.DMA,
        ],
        compiler_params=pltpu.CompilerParams(vmem_limit_bytes=MIRROR_VMEM_LIMIT),
        cost_estimate=pl.CostEstimate(flops=2_500_000_000, bytes_accessed=10_000_000, transcendentals=0),
        name="mirror",
    )(rank, left, received, direct)


def body(cycle_inter, integrals):
    x = jnp.swapaxes(cycle_inter, 0, 1)
    v = jnp.swapaxes(integrals, 0, 1)
    rank = lax.axis_index(AXES).astype(jnp.int32).reshape(1)
    received = lax.all_to_all(pack(rank, x, v), AXES, 0, 0, tiled=True)
    left, direct = local(rank, x, v)
    mine, other = mirror(rank, left, received, direct)
    rows = mine + lax.ppermute(other, "core", [(0, 1), (1, 0)])
    parts = jnp.broadcast_to(rows[:, None], (HALVES, COL_DEVICES, OUT_ROWS, LANES))
    parts = parts.reshape(HALVES * COL_DEVICES, OUT_ROWS, LANES)
    return jnp.sum(lax.all_to_all(parts, CHIPS, 0, 0, tiled=True), axis=0)


def solution(mesh):
    cores = Mesh(mesh.devices.reshape(HALVES, CORES, COL_DEVICES), AXES)
    return jax.shard_map(
        body,
        mesh=cores,
        in_specs=(P(None, AXES, None), P(None, AXES, None)),
        out_specs=P(("half", "core"), None),
        check_vma=False,
    )
```
